32 devices in a mesh: lat: 4 (over z), lon: 8 (over y, x, core).
Axes of the slice: x: 2, y: 2, z: 4, core: 2. Of those that a mesh axis runs over, the one named last changes fastest.
Arguments:
- tracer: float32 [64, 3600, 128], P('lat', 'lon'), may hold values from -6 to 6
- east_courant: float32 [64, 3600, 128], P('lat', 'lon'), may hold values from -0.3 to 0.3
- east_diffusion: float32 [64, 3600, 128], P('lat', 'lon'), may hold values from 0.05 to 0.2
- south_courant: float32 [64, 3600, 128], P('lat', 'lon'), may hold values from -0.3 to 0.3
- south_diffusion: float32 [64, 3600, 128], P('lat', 'lon'), may hold values from 0.05 to 0.2
- cutoff: int32 [64], replicated, may hold values from 1 to 1800, as said below
Outputs:
- advanced: float32 [64, 3600, 128], P('lat', 'lon')
The draws below stay inside these ranges and needn't reach their ends.
Inputs may be any that keep to these rules, and one draw needn't show every extreme that they name: Rows whose distance in rows from the nearer pole is 10 or more have cutoff 1800; all other rows have cutoffs below 1800, and the two rows at the poles have cutoff 1.
All inputs are finite; a program needn't handle non-finite values.
Results may differ from the reference program's by a relative error of at most 0.000098.
Values sent between devices are 32-bit elements; how exact they have to be, the bound alone decides.
A program may use at most 128 MiB of HBM per device.

```python
import math
import jax
import jax.numpy as jnp

NLON = 3600
LEV = 128
SUBSTEPS = 2
NLAT = 64
POLAR = 10


def cutoff_law(key):
    places = jnp.arange(NLAT, dtype=jnp.int32)
    distance = jnp.minimum(places, NLAT - 1 - places)
    highest = NLON // 2
    spread_top = max(2, highest // POLAR) + 2
    jitter = jax.random.randint(key, (NLAT,), 0, spread_top, dtype=jnp.int32)
    ramped = distance * highest // POLAR + jitter
    inside = jnp.clip(ramped, 1, highest - 1)
    inside = jnp.where(distance == 0, 1, inside)
    return jnp.where(distance < POLAR, inside, highest).astype(jnp.int32)


def draw_cutoff(key, part):
    return cutoff_law(jax.random.fold_in(key, 7))


def draw_tracer(key, part):
    cutoffs = cutoff_law(jax.random.fold_in(key, 7))
    columns = jnp.arange(NLON, dtype=jnp.int32)
    noise_key = jax.random.fold_in(key, 11)
    phase_key = jax.random.fold_in(key, 13)
    offsets = jax.random.uniform(phase_key, (2, NLAT, 1, LEV), jnp.float32, 0.0, 2.0 * math.pi)
    step_angle = 2.0 * math.pi / NLON
    first_phase = cutoffs[:, None] * columns[None, :] % NLON
    second_phase = (11 * cutoffs // 10)[:, None] * columns[None, :] % NLON
    first_wave = jnp.cos(first_phase.astype(jnp.float32)[:, :, None] * step_angle + offsets[0])
    second_wave = jnp.cos(second_phase.astype(jnp.float32)[:, :, None] * step_angle + offsets[1])
    polar_mask = (cutoffs < NLON // 2).astype(jnp.float32)[:, None, None]
    roughness = jax.random.normal(noise_key, (NLAT, NLON, LEV), jnp.float32)
    wave_sum = 2.5 * first_wave + 1.5 * second_wave
    return jnp.clip(roughness + polar_mask * wave_sum, -6.0, 6.0).astype(jnp.float32)


def shard_levels(rng, dims, shards, smallest, top_value):
    level = 1.0
    for dim, parts in shards:
        draws = jax.random.uniform(jax.random.fold_in(jax.random.fold_in(rng, 6), dim), (parts,), jnp.float32, smallest / len(shards), top_value / len(shards))
        level = level * jnp.repeat(jnp.exp(draws), dims[dim] // parts).reshape((-1,) + (1,) * (len(dims) - 1 - dim))
    return level


def setup_inputs(seed: int = 0) -> dict:
    key_list = jax.random.split(jax.random.key(seed), 7)
    return {
        "tracer": draw_tracer(jax.random.fold_in(key_list[6], 71), 0),
        "east_courant": jnp.clip(jax.random.uniform(key_list[1], (NLAT, NLON, LEV), jnp.float32, -0.3, 0.3) * shard_levels(key_list[1], (NLAT, NLON, LEV), ((0, 4), (1, 8)), -0.4, 0.0), -0.3, 0.3),
        "east_diffusion": jnp.clip(0.05 + 0.15 * jax.random.uniform(key_list[2], (NLAT, NLON, LEV), jnp.float32) ** shard_levels(key_list[2], (NLAT, NLON, LEV), ((0, 4), (1, 8)), -0.2, 0.2), 0.05, 0.2),
        "south_courant": jnp.clip(jax.random.uniform(key_list[3], (NLAT, NLON, LEV), jnp.float32, -0.3, 0.3) * shard_levels(key_list[3], (NLAT, NLON, LEV), ((0, 4), (1, 8)), -0.4, 0.0), -0.3, 0.3),
        "south_diffusion": jnp.clip(0.05 + 0.15 * jax.random.uniform(key_list[4], (NLAT, NLON, LEV), jnp.float32) ** shard_levels(key_list[4], (NLAT, NLON, LEV), ((0, 4), (1, 8)), -0.2, 0.2), 0.05, 0.2),
        "cutoff": draw_cutoff(jax.random.fold_in(key_list[6], 71), 0),
    }


def advance(field, east_speed, east_mix, south_speed, south_mix):
    east_flux = east_speed[:, :-1] * 0.5 * (field[:, :-1] + field[:, 1:]) - east_mix[:, :-1] * (field[:, 1:] - field[:, :-1])
    south_flux = south_speed[1:] * 0.5 * (field[:-1] + field[1:]) - south_mix[1:] * (field[1:] - field[:-1])
    across = east_flux[1:-1, 1:] - east_flux[1:-1, :-1]
    meridian = south_flux[1:, 1:-1] - south_flux[:-1, 1:-1]
    return field[1:-1, 1:-1] - across - meridian


def extend_full(values):
    beside_all = jnp.concatenate([values[:, -1:], values, values[:, :1]], 1)
    return jnp.pad(beside_all, ((1, 1), (0, 0), (0, 0)))


def reference(tracer, east_courant, east_diffusion, south_courant, south_diffusion, cutoff):
    places = jnp.arange(NLAT, dtype=jnp.int32)
    keeper = (places > 0).astype(jnp.float32)[:, None, None]
    east_speed = extend_full(east_courant)
    east_mix = extend_full(east_diffusion)
    south_speed = extend_full(south_courant * keeper)
    south_mix = extend_full(south_diffusion * keeper)
    field = tracer
    for substep in range(SUBSTEPS):
        field = advance(extend_full(field), east_speed, east_mix, south_speed, south_mix)
    spectrum = jnp.fft.rfft(field, axis=1)
    waves = jnp.arange(NLON // 2 + 1).astype(jnp.float32)
    levelled = cutoff.astype(jnp.float32)[:, None]
    damping = jnp.minimum(1.0, (levelled / jnp.maximum(waves, 1.0)[None, :]) ** 2)
    smoothed = jnp.fft.irfft(spectrum * damping[:, :, None], n=NLON, axis=1).astype(jnp.float32)
    polar_rows = (cutoff < NLON // 2)[:, None, None]
    return jnp.where(polar_rows, smoothed, field)
```

```python
import functools
import math

import jax
import jax.numpy as jnp
import ml_dtypes
import numpy as np
from jax import lax
from jax.experimental import pallas as pl
from jax.experimental.pallas import tpu as pltpu
from jax.sharding import PartitionSpec as P

SUBSTEPS = 2


def extended(block, sides, width, periodic):
    for axis, dim in sides:
        count = lax.axis_size(axis)
        forward = [(i, i + 1) for i in range(count - 1)]
        if periodic:
            forward.append((count - 1, 0))
        backward = [(target, source) for source, target in forward]
        low = lax.ppermute(
            lax.slice_in_dim(block, block.shape[dim] - width, None, axis=dim), axis, forward
        )
        high = lax.ppermute(lax.slice_in_dim(block, 0, width, axis=dim), axis, backward)
        block = jnp.concatenate([low, block, high], axis=dim)
    return block


def advance(field, east_speed, east_mix, south_speed, south_mix):
    east_flux = east_speed[:, :-1] * 0.5 * (field[:, :-1] + field[:, 1:]) - east_mix[:, :-1] * (
        field[:, 1:] - field[:, :-1]
    )
    south_flux = south_speed[1:] * 0.5 * (field[:-1] + field[1:]) - south_mix[1:] * (
        field[1:] - field[:-1]
    )
    across = east_flux[1:-1, 1:] - east_flux[1:-1, :-1]
    meridian = south_flux[1:, 1:-1] - south_flux[:-1, 1:-1]
    return field[1:-1, 1:-1] - across - meridian


def split_four(coefs, levels):
    return (
        coefs[:, :, :levels],
        coefs[:, :, levels : 2 * levels],
        coefs[:, :, 2 * levels : 3 * levels],
        coefs[:, :, 3 * levels :],
    )


def extend(values, depth):
    beside_all = extended(values, (("lon", 1),), depth, True)
    return extended(beside_all, (("lat", 0),), depth, False)


def angles(rows, cols, length):
    first = jnp.arange(rows, dtype=jnp.int32)
    second = jnp.arange(cols, dtype=jnp.int32)
    phase = first[:, None] * second[None, :] % length
    angle = phase.astype(jnp.float32) * (2.0 * math.pi / length)
    return (jnp.cos(angle), jnp.sin(angle))


def contract(form, values, table):
    return jnp.einsum(
        form, values, table, precision=lax.Precision.HIGHEST, preferred_element_type=jnp.float32
    )


def rotate(real, imag, cosine, sine, form, sign):
    new_real = contract(form, real, cosine) - sign * contract(form, imag, sine)
    new_imag = contract(form, imag, cosine) + sign * contract(form, real, sine)
    return (new_real, new_imag)


def pick_factor(length):
    factor = 1
    for candidate in range(1, int(math.isqrt(length)) + 1):
        if length % candidate == 0:
            factor = candidate
    return factor


def filter_rows_local(whole_rows, item_cut):
    share, length, levels = whole_rows.shape
    outer = pick_factor(length)
    inner = length // outer
    shaped = whole_rows.reshape(share, outer, inner, levels)
    cos_outer, sin_outer = angles(outer, outer, outer)
    cos_inner, sin_inner = angles(inner, inner, inner)
    cos_twist, sin_twist = angles(outer, inner, length)
    first_real = contract("janl,ak->jknl", shaped, cos_outer)
    first_imag = -contract("janl,ak->jknl", shaped, sin_outer)
    twist_real = cos_twist[None, :, :, None]
    twist_imag = sin_twist[None, :, :, None]
    turned_real = first_real * twist_real + first_imag * twist_imag
    turned_imag = first_imag * twist_real - first_real * twist_imag
    spec_real, spec_imag = rotate(
        turned_real, turned_imag, cos_inner, sin_inner, "jknl,nm->jkml", -1.0
    )
    low = jnp.arange(outer, dtype=jnp.int32)
    high = jnp.arange(inner, dtype=jnp.int32)
    wave = low[:, None] + outer * high[None, :]
    folded = jnp.minimum(wave, length - wave).astype(jnp.float32)
    levelled = item_cut.astype(jnp.float32)[:, None, None]
    damping = jnp.minimum(1.0, (levelled / jnp.maximum(folded, 1.0)[None, :, :]) ** 2) / length
    spec_real = spec_real * damping[:, :, :, None]
    spec_imag = spec_imag * damping[:, :, :, None]
    back_real, back_imag = rotate(spec_real, spec_imag, cos_inner, sin_inner, "jkml,nm->jknl", 1.0)
    unturned_real = back_real * twist_real - back_imag * twist_imag
    unturned_imag = back_imag * twist_real + back_real * twist_imag
    result = contract("jknl,ak->janl", unturned_real, cos_outer) - contract(
        "jknl,ak->janl", unturned_imag, sin_outer
    )
    return result.reshape(share, length, levels)


def smooth_rows(block, global_rows, cutoff):
    whole_rows = lax.all_to_all(block, "lon", split_axis=0, concat_axis=1, tiled=True)
    share = whole_rows.shape[0]
    length = whole_rows.shape[1]
    first = lax.axis_index("lon") * share
    item_row = lax.dynamic_slice_in_dim(global_rows, first, share, 0)
    matcher = item_row[:, None] == jnp.arange(cutoff.shape[0], dtype=jnp.int32)[None, :]
    item_cut = jnp.sum(jnp.where(matcher, cutoff[None, :], 0), axis=1)
    smoothed = filter_rows_local(whole_rows, item_cut)
    kept = jnp.where((item_cut < length // 2)[:, None, None], smoothed, whole_rows)
    return lax.all_to_all(kept, "lon", split_axis=1, concat_axis=0, tiled=True)


def on_device(tracer, east_courant, east_diffusion, south_courant, south_diffusion, cutoff):
    count, width, levels = tracer.shape
    lat_pos = lax.axis_index("lat")
    rows_here = lat_pos * count + jnp.arange(count, dtype=jnp.int32)
    keeper = (rows_here > 0).astype(jnp.float32)[:, None, None]
    coefs = jnp.concatenate(
        [east_courant, east_diffusion, south_courant * keeper, south_diffusion * keeper], 2
    )
    field = tracer
    coef_ext = extend(coefs, 1)
    for substep in range(SUBSTEPS):
        field = advance(extend(field, 1), *split_four(coef_ext, levels))
    field = smooth_rows(field, rows_here, cutoff)
    return field


MESH = pl.DeviceIdType.MESH


def padded(length):
    return -(-length // 16) * 16


def split_bf16(values):
    high = values.astype(ml_dtypes.bfloat16)
    low = (values - high.astype(np.float64)).astype(ml_dtypes.bfloat16)
    return high, low


def tables(parts, width):
    tall = padded(width)
    place = np.arange(width)
    angle = (place[:, None] * place[None, :] % width) * (2.0 * np.pi / width)
    stack = np.zeros((4, tall, tall), ml_dtypes.bfloat16)
    cos_high, cos_low = split_bf16(np.cos(angle))
    sin_high, sin_low = split_bf16(np.sin(angle))
    for index, table in enumerate((cos_high, sin_high, cos_low, sin_low)):
        stack[index, :width, :width] = table
    half = parts // 2 + 1
    turn = np.arange(half)[:, None] * place[None, :] * (2.0 * np.pi / (parts * width))
    twist = np.zeros((2, half, tall, 128), np.float32)
    twist[0, :, :width] = np.cos(turn)[:, :, None]
    twist[1, :, :width] = np.sin(turn)[:, :, None]
    return stack.reshape(4 * tall, tall), twist


def block_kernel(
    rows, width, parts, bands, polar,
    cut_ref, f_in, ec_in, ed_in, sc_in, sd_in, dft_in, tw_in, out,
    f0, f1, ec, ed, sc, sd, dft, tw, whole, spec,
    to_east0, to_west0, to_east1, to_west1, from_west0, from_east0, from_west1, from_east1,
    load_sem, lon_send, lon_recv, z_send, z_recv, go_send, go_recv, back_send, back_recv, out_sem,
):
    me = lax.axis_index("lon")
    lat = lax.axis_index("lat")
    east = lax.rem(me + 1, parts)
    west = lax.rem(me + parts - 1, parts)
    has_south = lat > 0
    has_north = lat < bands - 1
    is_polar = jnp.logical_or(lat == 0, lat == bands - 1)
    base = jnp.where(lat == 0, 0, rows - polar)
    tall = padded(width)
    half = parts // 2 + 1

    loads = [
        pltpu.make_async_copy(f_in, f0.at[pl.ds(1, rows)], load_sem.at[0]),
        pltpu.make_async_copy(ec_in, ec, load_sem.at[1]),
        pltpu.make_async_copy(ed_in, ed, load_sem.at[2]),
        pltpu.make_async_copy(sc_in, sc.at[pl.ds(0, rows)], load_sem.at[3]),
        pltpu.make_async_copy(sd_in, sd.at[pl.ds(0, rows)], load_sem.at[4]),
        pltpu.make_async_copy(dft_in, dft, load_sem.at[5]),
        pltpu.make_async_copy(tw_in, tw, load_sem.at[6]),
    ]
    for load in loads:
        load.start()

    barrier = pltpu.get_barrier_semaphore()
    for step in range(1, parts):
        pl.semaphore_signal(
            barrier, 1, device_id={"lon": lax.rem(me + step, parts)}, device_id_type=MESH
        )

    @pl.when(has_south)
    def _():
        pl.semaphore_signal(barrier, 1, device_id={"lat": lat - 1}, device_id_type=MESH)

    @pl.when(has_north)
    def _():
        pl.semaphore_signal(barrier, 1, device_id={"lat": lat + 1}, device_id_type=MESH)

    peers = parts - 1 + jnp.where(has_south, 1, 0) + jnp.where(has_north, 1, 0)
    pl.semaphore_wait(barrier, peers)

    def remote(src, dst, send, recv, where):
        return pltpu.make_async_remote_copy(
            src_ref=src, dst_ref=dst, send_sem=send, recv_sem=recv,
            device_id=where, device_id_type=MESH,
        )

    north = {"lat": lax.rem(lat + 1, bands)}
    south = {"lat": lax.rem(lat + bands - 1, bands)}
    up0 = remote(f_in.at[rows - 1], f0.at[0], z_send.at[0], z_recv.at[0], north)
    down0 = [
        remote(f_in.at[0], f0.at[rows + 1], z_send.at[1], z_recv.at[1], south),
        remote(sc_in.at[0], sc.at[rows], z_send.at[2], z_recv.at[2], south),
        remote(sd_in.at[0], sd.at[rows], z_send.at[3], z_recv.at[3], south),
    ]
    up1 = remote(f1.at[rows], f1.at[0], z_send.at[4], z_recv.at[4], north)
    down1 = remote(f1.at[1], f1.at[rows + 1], z_send.at[5], z_recv.at[5], south)
    east0 = remote(to_east0, from_west0, lon_send.at[0], lon_recv.at[0], {"lon": east})
    west0 = remote(to_west0, from_east0, lon_send.at[1], lon_recv.at[1], {"lon": west})
    east1 = remote(to_east1, from_west1, lon_send.at[2], lon_recv.at[2], {"lon": east})
    west1 = remote(to_west1, from_east1, lon_send.at[3], lon_recv.at[3], {"lon": west})

    @pl.when(has_north)
    def _():
        up0.start()

    @pl.when(has_south)
    def _():
        for copy in down0:
            copy.start()

    for load in loads[:3]:
        load.wait()

    @pl.loop(0, rows)
    def _(j):
        to_east0[0, j] = f0[j + 1, width - 1 : width, :]
        to_east0[1, j] = ec[j, width - 1 : width, :]
        to_east0[2, j] = ed[j, width - 1 : width, :]
        to_west0[j] = f0[j + 1, 0:1, :]

    east0.start()
    west0.start()
    loads[3].wait()
    loads[4].wait()
    nothing = jnp.zeros((width, 128), jnp.float32)

    @pl.when(lat == 0)
    def _():
        f0[0] = nothing
        f1[0] = nothing
        sc[0] = nothing
        sd[0] = nothing

    @pl.when(lat == bands - 1)
    def _():
        f0[rows + 1] = nothing
        f1[rows + 1] = nothing
        sc[rows] = nothing
        sd[rows] = nothing

    def advance_row(src, dst, j, west_col, east_col):
        value = src[j + 1]
        beside = jnp.concatenate([value[1:], east_col[j]], axis=0)
        flux = ec[j] * 0.5 * (value + beside) - ed[j] * (beside - value)
        edge = west_col[j]
        first = value[0:1]
        entering = from_west0[1, j] * 0.5 * (edge + first) - from_west0[2, j] * (first - edge)
        flux_west = jnp.concatenate([entering, flux[:-1]], axis=0)
        below = src[j]
        above = src[j + 2]
        flux_south = sc[j] * 0.5 * (below + value) - sd[j] * (value - below)
        flux_north = sc[j + 1] * 0.5 * (value + above) - sd[j + 1] * (above - value)
        dst[j + 1] = value - (flux - flux_west) - (flux_north - flux_south)

    def wait_z0():
        @pl.when(has_south)
        def _():
            up0.wait_recv()

        @pl.when(has_north)
        def _():
            for copy in down0:
                copy.wait_recv()

    def wait_z1():
        @pl.when(has_south)
        def _():
            up1.wait_recv()

        @pl.when(has_north)
        def _():
            down1.wait_recv()

    @pl.when(jnp.logical_not(is_polar))
    def _():
        wait_z0()

    east0.wait_recv()
    west0.wait_recv()
    ascending = lat < bands // 2

    @pl.loop(0, rows)
    def _(t):
        j = jnp.where(ascending, t, rows - 1 - t)

        @pl.when(jnp.logical_and(is_polar, t == rows - 1))
        def _():
            wait_z0()

        advance_row(f0, f1, j, from_west0.at[0], from_east0)
        to_east1[j] = f1[j + 1, width - 1 : width, :]
        to_west1[j] = f1[j + 1, 0:1, :]

    east1.start()
    west1.start()

    @pl.when(has_north)
    def _():
        up1.start()

    @pl.when(has_south)
    def _():
        down1.start()

    east1.wait_recv()
    west1.wait_recv()

    def owner_of(r):
        return jnp.where(r < parts, r, (r - parts) * (parts - 1))

    def go_copy(r, j):
        slot = r // parts
        return remote(
            f0.at[j + 1], whole.at[slot, me], go_send.at[r], go_recv.at[slot, me],
            {"lon": owner_of(r)},
        )

    def go_local(r, j):
        slot = r // parts
        return pltpu.make_async_copy(f0.at[j + 1], whole.at[slot, me], go_send.at[r])

    def filter_slot(slot, r):
        for step in range(1, parts):
            source = lax.rem(me + step, parts)
            remote(
                f0.at[1], whole.at[slot, source], go_send.at[r], go_recv.at[slot, source],
                {"lon": source},
            ).wait_recv()
        go_local(r, base + r).wait()
        extra = jnp.zeros((tall - width, 128), jnp.float32)
        pieces = [whole[slot, a] for a in range(parts)]
        for q in range(half):
            real, imag = None, None
            for a in range(parts // 2):
                merged = (
                    pieces[a] + pieces[a + parts // 2] if q % 2 == 0 else pieces[a] - pieces[a + parts // 2]
                )
                turn = 2.0 * math.pi * ((a * q) % parts) / parts
                cosine, sine = math.cos(turn), math.sin(turn)
                if abs(cosine) > 1e-9:
                    term = merged if cosine > 1 - 1e-9 else merged * cosine
                    real = term if real is None else real + term
                if abs(sine) > 1e-9:
                    term = merged * (-sine)
                    imag = term if imag is None else imag + term
            real = jnp.concatenate([real, extra], axis=0)
            if imag is None:
                new_real = real * tw[0, q]
                new_imag = -real * tw[1, q]
            else:
                imag = jnp.concatenate([imag, extra], axis=0)
                new_real = real * tw[0, q] + imag * tw[1, q]
                new_imag = imag * tw[0, q] - real * tw[1, q]
            spec[q, :, 0:128] = new_real
            spec[q, :, 128:256] = new_imag

        cut = cut_ref[lat * rows + base + r].astype(jnp.float32)
        length = parts * width

        def products(values):
            high = values.astype(jnp.bfloat16)
            low = (values - high.astype(jnp.float32)).astype(jnp.bfloat16)
            main = jnp.dot(dft[...], high, preferred_element_type=jnp.float32)
            rest = jnp.dot(dft[0 : 2 * tall, :], low, preferred_element_type=jnp.float32)
            by_cos = main[0:tall] + (main[2 * tall : 3 * tall] + rest[0:tall])
            by_sin = main[tall : 2 * tall] + (main[3 * tall : 4 * tall] + rest[tall : 2 * tall])
            return by_cos, by_sin

        @pl.loop(0, half)
        def _(q):
            by_cos, by_sin = products(spec[q])
            real = by_cos[:, 0:128] + by_sin[:, 128:256]
            imag = by_cos[:, 128:256] - by_sin[:, 0:128]
            wave = q + parts * lax.broadcasted_iota(jnp.int32, (tall, 128), 0)
            folded = jnp.maximum(jnp.minimum(wave, length - wave), 1).astype(jnp.float32)
            ratio = cut / folded
            damping = jnp.minimum(1.0, ratio * ratio) * (1.0 / length)
            both = jnp.concatenate([real * damping, imag * damping], axis=1)
            by_cos, by_sin = products(both)
            real = by_cos[:, 0:128] - by_sin[:, 128:256]
            imag = by_cos[:, 128:256] + by_sin[:, 0:128]
            spec[q, :, 0:128] = real * tw[0, q] - imag * tw[1, q]
            spec[q, :, 128:256] = imag * tw[0, q] + real * tw[1, q]

        for a in range(parts):
            total = spec[0, 0:width, 0:128]
            for q in range(1, half):
                turn = 2.0 * math.pi * ((a * q) % parts) / parts
                weight = 1.0 if q == parts // 2 else 2.0
                cosine, sine = weight * math.cos(turn), weight * math.sin(turn)
                if abs(cosine) > 1e-9:
                    total = total + spec[q, 0:width, 0:128] * cosine
                if abs(sine) > 1e-9:
                    total = total - spec[q, 0:width, 128:256] * sine
            whole[slot, a] = total
        for step in range(1, parts):
            target = lax.rem(me + step, parts)
            remote(
                whole.at[slot, target], out.at[base + r], back_send.at[slot, step],
                back_recv.at[r], {"lon": target},
            ).start()
        pltpu.make_async_copy(whole.at[slot, me], out.at[base + r], back_recv.at[r]).start()

    @pl.when(is_polar)
    def _():
        @pl.loop(0, polar)
        def _(t):
            r = lax.rem(me + t, polar)
            j = base + r
            advance_row(f1, f0, j, from_west1, from_east1)

            @pl.when(owner_of(r) == me)
            def _():
                go_local(r, j).start()

            @pl.when(owner_of(r) != me)
            def _():
                go_copy(r, j).start()

        wait_z1()
        rest = jnp.where(lat == 0, polar, 0)

        @pl.loop(0, rows - polar)
        def _(t):
            advance_row(f1, f0, rest + t, from_west1, from_east1)

        keep = pltpu.make_async_copy(
            f0.at[pl.ds(rest + 1, rows - polar)], out.at[pl.ds(rest, rows - polar)], out_sem
        )
        keep.start()
        loads[5].wait()
        loads[6].wait()
        filter_slot(0, me)

        @pl.loop(parts, polar)
        def _(r):
            @pl.when(owner_of(r) == me)
            def _():
                filter_slot(1, r)

        keep.wait()

        @pl.loop(0, polar)
        def _(r):
            slot = r // parts

            @pl.when(owner_of(r) != me)
            def _():
                go_copy(r, base + r).wait_send()
                remote(
                    whole.at[slot, me], out.at[base + r], back_send.at[slot, 0],
                    back_recv.at[r], {"lon": east},
                ).wait_recv()

            @pl.when(owner_of(r) == me)
            def _():
                for step in range(1, parts):
                    target = lax.rem(me + step, parts)
                    remote(
                        whole.at[slot, target], out.at[base + r], back_send.at[slot, step],
                        back_recv.at[r], {"lon": target},
                    ).wait_send()
                pltpu.make_async_copy(
                    whole.at[slot, me], out.at[base + r], back_recv.at[r]
                ).wait()

    @pl.when(jnp.logical_not(is_polar))
    def _():
        wait_z1()

        @pl.loop(0, rows)
        def _(t):
            advance_row(f1, f0, t, from_west1, from_east1)

        keep = pltpu.make_async_copy(f0.at[pl.ds(1, rows)], out, out_sem)
        keep.start()
        loads[5].wait()
        loads[6].wait()
        keep.wait()

    for copy in (east0, west0, east1, west1):
        copy.wait_send()

    @pl.when(has_north)
    def _():
        up0.wait_send()
        up1.wait_send()

    @pl.when(has_south)
    def _():
        for copy in down0:
            copy.wait_send()
        down1.wait_send()


def on_block(mesh, polar, tracer, east_courant, east_diffusion, south_courant, south_diffusion, cutoff):
    rows, width, levels = tracer.shape
    parts, bands = mesh.shape["lon"], mesh.shape["lat"]
    tall, half = padded(width), parts // 2 + 1
    stack, twist = tables(parts, width)
    hbm = pl.BlockSpec(memory_space=pl.ANY)
    field = lambda count: pltpu.VMEM((count, width, levels), jnp.float32)
    edge = pltpu.VMEM((rows, 1, levels), jnp.float32)
    edge3 = pltpu.VMEM((3, rows, 1, levels), jnp.float32)
    slots = -(-polar // parts)
    dma = lambda *shape: pltpu.SemaphoreType.DMA(shape)
    return pl.pallas_call(
        functools.partial(block_kernel, rows, width, parts, bands, polar),
        out_shape=jax.ShapeDtypeStruct(tracer.shape, jnp.float32),
        in_specs=[pl.BlockSpec(memory_space=pltpu.SMEM)] + [hbm] * 7,
        out_specs=hbm,
        scratch_shapes=[
            field(rows + 2), field(rows + 2), field(rows), field(rows), field(rows + 1), field(rows + 1),
            pltpu.VMEM(stack.shape, jnp.bfloat16),
            pltpu.VMEM(twist.shape, jnp.float32),
            pltpu.VMEM((slots, parts, width, levels), jnp.float32),
            pltpu.VMEM((half, tall, 2 * levels), jnp.float32),
            edge3, edge, edge, edge, edge3, edge, edge, edge,
            dma(7), dma(4), dma(4), dma(6), dma(6), dma(polar), dma(slots, parts),
            dma(slots, parts), dma(polar), pltpu.SemaphoreType.DMA,
        ],
        compiler_params=pltpu.CompilerParams(
            collective_id=0, has_side_effects=True, vmem_limit_bytes=60 * 2**20
        ),
    )(
        cutoff, tracer, east_courant, east_diffusion, south_courant, south_diffusion,
        jnp.asarray(stack), jnp.asarray(twist),
    )


def solution(mesh):
    in_specs = (P("lat", "lon", None),) * 5 + (P(),)
    out_specs = P("lat", "lon", None)
    parts, bands = mesh.shape["lon"], mesh.shape["lat"]

    def run(tracer, *others):
        polar = tracer.shape[0] // 6
        rows = tracer.shape[0] // bands
        fits = (
            bands > 2
            and polar + SUBSTEPS <= rows
            and parts <= polar <= parts + 2
            and parts % 8 == 0
            and tracer.shape[2] == 128
        )
        body = functools.partial(on_block, mesh, polar) if fits else on_device
        return jax.shard_map(
            body, mesh=mesh, in_specs=in_specs, out_specs=out_specs, check_vma=False
        )(tracer, *others)

    return run
```

```python
import functools
import math

import jax
import jax.numpy as jnp
import ml_dtypes
import numpy as np
from jax import lax
from jax.experimental import pallas as pl
from jax.experimental.pallas import tpu as pltpu
from jax.sharding import PartitionSpec as P

SUBSTEPS = 2


def extended(block, sides, width, periodic):
    for axis, dim in sides:
        count = lax.axis_size(axis)
        forward = [(i, i + 1) for i in range(count - 1)]
        if periodic:
            forward.append((count - 1, 0))
        backward = [(target, source) for source, target in forward]
        low = lax.ppermute(
            lax.slice_in_dim(block, block.shape[dim] - width, None, axis=dim), axis, forward
        )
        high = lax.ppermute(lax.slice_in_dim(block, 0, width, axis=dim), axis, backward)
        block = jnp.concatenate([low, block, high], axis=dim)
    return block


def advance(field, east_speed, east_mix, south_speed, south_mix):
    east_flux = east_speed[:, :-1] * 0.5 * (field[:, :-1] + field[:, 1:]) - east_mix[:, :-1] * (
        field[:, 1:] - field[:, :-1]
    )
    south_flux = south_speed[1:] * 0.5 * (field[:-1] + field[1:]) - south_mix[1:] * (
        field[1:] - field[:-1]
    )
    across = east_flux[1:-1, 1:] - east_flux[1:-1, :-1]
    meridian = south_flux[1:, 1:-1] - south_flux[:-1, 1:-1]
    return field[1:-1, 1:-1] - across - meridian


def split_four(coefs, levels):
    return (
        coefs[:, :, :levels],
        coefs[:, :, levels : 2 * levels],
        coefs[:, :, 2 * levels : 3 * levels],
        coefs[:, :, 3 * levels :],
    )


def extend(values, depth):
    beside_all = extended(values, (("lon", 1),), depth, True)
    return extended(beside_all, (("lat", 0),), depth, False)


def angles(rows, cols, length):
    first = jnp.arange(rows, dtype=jnp.int32)
    second = jnp.arange(cols, dtype=jnp.int32)
    phase = first[:, None] * second[None, :] % length
    angle = phase.astype(jnp.float32) * (2.0 * math.pi / length)
    return (jnp.cos(angle), jnp.sin(angle))


def contract(form, values, table):
    return jnp.einsum(
        form, values, table, precision=lax.Precision.HIGHEST, preferred_element_type=jnp.float32
    )


def rotate(real, imag, cosine, sine, form, sign):
    new_real = contract(form, real, cosine) - sign * contract(form, imag, sine)
    new_imag = contract(form, imag, cosine) + sign * contract(form, real, sine)
    return (new_real, new_imag)


def pick_factor(length):
    factor = 1
    for candidate in range(1, int(math.isqrt(length)) + 1):
        if length % candidate == 0:
            factor = candidate
    return factor


def filter_rows_local(whole_rows, item_cut):
    share, length, levels = whole_rows.shape
    outer = pick_factor(length)
    inner = length // outer
    shaped = whole_rows.reshape(share, outer, inner, levels)
    cos_outer, sin_outer = angles(outer, outer, outer)
    cos_inner, sin_inner = angles(inner, inner, inner)
    cos_twist, sin_twist = angles(outer, inner, length)
    first_real = contract("janl,ak->jknl", shaped, cos_outer)
    first_imag = -contract("janl,ak->jknl", shaped, sin_outer)
    twist_real = cos_twist[None, :, :, None]
    twist_imag = sin_twist[None, :, :, None]
    turned_real = first_real * twist_real + first_imag * twist_imag
    turned_imag = first_imag * twist_real - first_real * twist_imag
    spec_real, spec_imag = rotate(
        turned_real, turned_imag, cos_inner, sin_inner, "jknl,nm->jkml", -1.0
    )
    low = jnp.arange(outer, dtype=jnp.int32)
    high = jnp.arange(inner, dtype=jnp.int32)
    wave = low[:, None] + outer * high[None, :]
    folded = jnp.minimum(wave, length - wave).astype(jnp.float32)
    levelled = item_cut.astype(jnp.float32)[:, None, None]
    damping = jnp.minimum(1.0, (levelled / jnp.maximum(folded, 1.0)[None, :, :]) ** 2) / length
    spec_real = spec_real * damping[:, :, :, None]
    spec_imag = spec_imag * damping[:, :, :, None]
    back_real, back_imag = rotate(spec_real, spec_imag, cos_inner, sin_inner, "jkml,nm->jknl", 1.0)
    unturned_real = back_real * twist_real - back_imag * twist_imag
    unturned_imag = back_imag * twist_real + back_real * twist_imag
    result = contract("jknl,ak->janl", unturned_real, cos_outer) - contract(
        "jknl,ak->janl", unturned_imag, sin_outer
    )
    return result.reshape(share, length, levels)


def smooth_rows(block, global_rows, cutoff):
    whole_rows = lax.all_to_all(block, "lon", split_axis=0, concat_axis=1, tiled=True)
    share = whole_rows.shape[0]
    length = whole_rows.shape[1]
    first = lax.axis_index("lon") * share
    item_row = lax.dynamic_slice_in_dim(global_rows, first, share, 0)
    matcher = item_row[:, None] == jnp.arange(cutoff.shape[0], dtype=jnp.int32)[None, :]
    item_cut = jnp.sum(jnp.where(matcher, cutoff[None, :], 0), axis=1)
    smoothed = filter_rows_local(whole_rows, item_cut)
    kept = jnp.where((item_cut < length // 2)[:, None, None], smoothed, whole_rows)
    return lax.all_to_all(kept, "lon", split_axis=1, concat_axis=0, tiled=True)


def on_device(tracer, east_courant, east_diffusion, south_courant, south_diffusion, cutoff):
    count, width, levels = tracer.shape
    lat_pos = lax.axis_index("lat")
    rows_here = lat_pos * count + jnp.arange(count, dtype=jnp.int32)
    keeper = (rows_here > 0).astype(jnp.float32)[:, None, None]
    coefs = jnp.concatenate(
        [east_courant, east_diffusion, south_courant * keeper, south_diffusion * keeper], 2
    )
    field = tracer
    coef_ext = extend(coefs, 1)
    for substep in range(SUBSTEPS):
        field = advance(extend(field, 1), *split_four(coef_ext, levels))
    field = smooth_rows(field, rows_here, cutoff)
    return field


MESH = pl.DeviceIdType.MESH


def padded(length):
    return -(-length // 16) * 16


def split_bf16(values):
    high = values.astype(ml_dtypes.bfloat16)
    low = (values - high.astype(np.float64)).astype(ml_dtypes.bfloat16)
    return high, low


def tables(parts, width):
    tall = padded(width)
    place = np.arange(width)
    angle = (place[:, None] * place[None, :] % width) * (2.0 * np.pi / width)
    stack = np.zeros((4, tall, tall), ml_dtypes.bfloat16)
    cos_high, cos_low = split_bf16(np.cos(angle))
    sin_high, sin_low = split_bf16(np.sin(angle))
    for index, table in enumerate((cos_high, sin_high, cos_low, sin_low)):
        stack[index, :width, :width] = table
    half = parts // 2 + 1
    turn = np.arange(half)[:, None] * place[None, :] * (2.0 * np.pi / (parts * width))
    twist = np.zeros((2, half, tall, 128), np.float32)
    twist[0, :, :width] = np.cos(turn)[:, :, None]
    twist[1, :, :width] = np.sin(turn)[:, :, None]
    return stack.reshape(4 * tall, tall), twist


def block_kernel(
    rows, width, parts, bands, polar,
    cut_ref, f_in, ec_in, ed_in, sc_in, sd_in, dft_in, tw_in, out,
    f0, f1, ec, ed, sc, sd, dft, tw, whole, spec,
    to_east1, to_west1, from_west0, from_east0, from_west1, from_east1,
    load_sem, table_sem, lon_send, lon_recv, z_send, z_recv, go_send, go_recv, back_send, back_recv, out_sem,
):
    me = lax.axis_index("lon")
    lat = lax.axis_index("lat")
    east = lax.rem(me + 1, parts)
    west = lax.rem(me + parts - 1, parts)
    has_south = lat > 0
    has_north = lat < bands - 1
    is_polar = jnp.logical_or(lat == 0, lat == bands - 1)
    base = jnp.where(lat == 0, 0, rows - polar)
    tall = padded(width)
    half = parts // 2 + 1

    ascending = lat < bands // 2

    def place(t):
        return jnp.where(ascending, t, rows - 1 - t)

    def load_row(j):
        return [
            pltpu.make_async_copy(src.at[:, j, :], dst.at[j + shift], load_sem.at[index, j])
            for index, (src, dst, shift) in enumerate(
                ((f_in, f0, 1), (ec_in, ec, 0), (ed_in, ed, 0), (sc_in, sc, 0), (sd_in, sd, 0))
            )
        ]

    @pl.loop(0, rows)
    def _(t):
        for load in load_row(place(t)):
            load.start()

    table_loads = [
        pltpu.make_async_copy(dft_in, dft, table_sem.at[0]),
        pltpu.make_async_copy(tw_in, tw, table_sem.at[1]),
    ]
    for load in table_loads:
        load.start()

    barrier = pltpu.get_barrier_semaphore()
    for step in range(1, parts):
        pl.semaphore_signal(
            barrier, 1, device_id={"lon": lax.rem(me + step, parts)}, device_id_type=MESH
        )

    @pl.when(has_south)
    def _():
        pl.semaphore_signal(barrier, 1, device_id={"lat": lat - 1}, device_id_type=MESH)

    @pl.when(has_north)
    def _():
        pl.semaphore_signal(barrier, 1, device_id={"lat": lat + 1}, device_id_type=MESH)

    peers = parts - 1 + jnp.where(has_south, 1, 0) + jnp.where(has_north, 1, 0)
    pl.semaphore_wait(barrier, peers)

    def remote(src, dst, send, recv, where):
        return pltpu.make_async_remote_copy(
            src_ref=src, dst_ref=dst, send_sem=send, recv_sem=recv,
            device_id=where, device_id_type=MESH,
        )

    north = {"lat": lax.rem(lat + 1, bands)}
    south = {"lat": lax.rem(lat + bands - 1, bands)}
    up0 = remote(f_in.at[:, rows - 1, :], f0.at[0], z_send.at[0], z_recv.at[0], north)
    down0 = [
        remote(f_in.at[:, 0, :], f0.at[rows + 1], z_send.at[1], z_recv.at[1], south),
        remote(sc_in.at[:, 0, :], sc.at[rows], z_send.at[2], z_recv.at[2], south),
        remote(sd_in.at[:, 0, :], sd.at[rows], z_send.at[3], z_recv.at[3], south),
    ]
    up1 = remote(f1.at[rows], f1.at[0], z_send.at[4], z_recv.at[4], north)
    down1 = remote(f1.at[1], f1.at[rows + 1], z_send.at[5], z_recv.at[5], south)
    edges0 = [
        remote(f_in.at[width - 1], from_west0.at[0], lon_send.at[0], lon_recv.at[0], {"lon": east}),
        remote(ec_in.at[width - 1], from_west0.at[1], lon_send.at[1], lon_recv.at[1], {"lon": east}),
        remote(ed_in.at[width - 1], from_west0.at[2], lon_send.at[4], lon_recv.at[4], {"lon": east}),
        remote(f_in.at[0], from_east0, lon_send.at[5], lon_recv.at[5], {"lon": west}),
    ]
    east1 = remote(to_east1, from_west1, lon_send.at[2], lon_recv.at[2], {"lon": east})
    west1 = remote(to_west1, from_east1, lon_send.at[3], lon_recv.at[3], {"lon": west})

    for copy in edges0:
        copy.start()

    @pl.when(has_north)
    def _():
        up0.start()

    @pl.when(has_south)
    def _():
        for copy in down0:
            copy.start()

    for load in load_row(place(0)):
        load.wait()
    nothing = jnp.zeros((width, 128), jnp.float32)

    @pl.when(lat == 0)
    def _():
        f0[0] = nothing
        f1[0] = nothing
        sc[0] = nothing
        sd[0] = nothing

    @pl.when(lat == bands - 1)
    def _():
        f0[rows + 1] = nothing
        f1[rows + 1] = nothing
        sc[rows] = nothing
        sd[rows] = nothing

    def advance_row(src, dst, j, west_col, east_col):
        value = src[j + 1]
        beside = jnp.concatenate([value[1:], east_col[pl.ds(j, 1), :]], axis=0)
        flux = ec[j] * 0.5 * (value + beside) - ed[j] * (beside - value)
        edge = west_col[pl.ds(j, 1), :]
        first = value[0:1]
        entering = from_west0[1, pl.ds(j, 1), :] * 0.5 * (edge + first) - from_west0[2, pl.ds(j, 1), :] * (first - edge)
        flux_west = jnp.concatenate([entering, flux[:-1]], axis=0)
        below = src[j]
        above = src[j + 2]
        flux_south = sc[j] * 0.5 * (below + value) - sd[j] * (value - below)
        flux_north = sc[j + 1] * 0.5 * (value + above) - sd[j + 1] * (above - value)
        dst[j + 1] = value - (flux - flux_west) - (flux_north - flux_south)

    def wait_z0():
        @pl.when(has_south)
        def _():
            up0.wait_recv()

        @pl.when(has_north)
        def _():
            for copy in down0:
                copy.wait_recv()

    def wait_z1():
        @pl.when(has_south)
        def _():
            up1.wait_recv()

        @pl.when(has_north)
        def _():
            down1.wait_recv()

    @pl.when(jnp.logical_not(is_polar))
    def _():
        wait_z0()

    for copy in edges0:
        copy.wait_recv()

    @pl.loop(0, rows)
    def _(t):
        j = place(t)

        @pl.when(t < rows - 1)
        def _():
            for load in load_row(place(t + 1)):
                load.wait()

        @pl.when(jnp.logical_and(is_polar, t == rows - 1))
        def _():
            wait_z0()

        advance_row(f0, f1, j, from_west0.at[0], from_east0)
        to_east1[pl.ds(j, 1), :] = f1[j + 1, width - 1 : width, :]
        to_west1[pl.ds(j, 1), :] = f1[j + 1, 0:1, :]

    east1.start()
    west1.start()

    @pl.when(has_north)
    def _():
        up1.start()

    @pl.when(has_south)
    def _():
        down1.start()

    east1.wait_recv()
    west1.wait_recv()

    def keep_row(j):
        return pltpu.make_async_copy(f0.at[j + 1], out.at[:, j, :], out_sem.at[j])

    def owner_of(r):
        return jnp.where(r < parts, r, (r - parts) * (parts - 1))

    def go_copy(r, j):
        slot = r // parts
        return remote(
            f0.at[j + 1], whole.at[slot, me], go_send.at[r], go_recv.at[slot, me],
            {"lon": owner_of(r)},
        )

    def go_local(r, j):
        slot = r // parts
        return pltpu.make_async_copy(f0.at[j + 1], whole.at[slot, me], go_send.at[r])

    def filter_slot(slot, r):
        for step in range(1, parts):
            source = lax.rem(me + step, parts)
            remote(
                f0.at[1], whole.at[slot, source], go_send.at[r], go_recv.at[slot, source],
                {"lon": source},
            ).wait_recv()
        go_local(r, base + r).wait()
        extra = jnp.zeros((tall - width, 128), jnp.float32)
        pieces = [whole[slot, a] for a in range(parts)]
        for q in range(half):
            real, imag = None, None
            for a in range(parts // 2):
                merged = (
                    pieces[a] + pieces[a + parts // 2] if q % 2 == 0 else pieces[a] - pieces[a + parts // 2]
                )
                turn = 2.0 * math.pi * ((a * q) % parts) / parts
                cosine, sine = math.cos(turn), math.sin(turn)
                if abs(cosine) > 1e-9:
                    term = merged if cosine > 1 - 1e-9 else merged * cosine
                    real = term if real is None else real + term
                if abs(sine) > 1e-9:
                    term = merged * (-sine)
                    imag = term if imag is None else imag + term
            real = jnp.concatenate([real, extra], axis=0)
            if imag is None:
                new_real = real * tw[0, q]
                new_imag = -real * tw[1, q]
            else:
                imag = jnp.concatenate([imag, extra], axis=0)
                new_real = real * tw[0, q] + imag * tw[1, q]
                new_imag = imag * tw[0, q] - real * tw[1, q]
            spec[q, :, 0:128] = new_real
            spec[q, :, 128:256] = new_imag

        cut = cut_ref[lat * rows + base + r].astype(jnp.float32)
        length = parts * width

        def products(values):
            high = values.astype(jnp.bfloat16)
            low = (values - high.astype(jnp.float32)).astype(jnp.bfloat16)
            main = jnp.dot(dft[...], high, preferred_element_type=jnp.float32)
            rest = jnp.dot(dft[0 : 2 * tall, :], low, preferred_element_type=jnp.float32)
            by_cos = main[0:tall] + (main[2 * tall : 3 * tall] + rest[0:tall])
            by_sin = main[tall : 2 * tall] + (main[3 * tall : 4 * tall] + rest[tall : 2 * tall])
            return by_cos, by_sin

        @pl.loop(0, half)
        def _(q):
            by_cos, by_sin = products(spec[q])
            real = by_cos[:, 0:128] + by_sin[:, 128:256]
            imag = by_cos[:, 128:256] - by_sin[:, 0:128]
            wave = q + parts * lax.broadcasted_iota(jnp.int32, (tall, 128), 0)
            folded = jnp.maximum(jnp.minimum(wave, length - wave), 1).astype(jnp.float32)
            ratio = cut / folded
            damping = jnp.minimum(1.0, ratio * ratio) * (1.0 / length)
            both = jnp.concatenate([real * damping, imag * damping], axis=1)
            by_cos, by_sin = products(both)
            real = by_cos[:, 0:128] - by_sin[:, 128:256]
            imag = by_cos[:, 128:256] + by_sin[:, 0:128]
            spec[q, :, 0:128] = real * tw[0, q] - imag * tw[1, q]
            spec[q, :, 128:256] = imag * tw[0, q] + real * tw[1, q]

        for a in range(parts):
            total = spec[0, 0:width, 0:128]
            for q in range(1, half):
                turn = 2.0 * math.pi * ((a * q) % parts) / parts
                weight = 1.0 if q == parts // 2 else 2.0
                cosine, sine = weight * math.cos(turn), weight * math.sin(turn)
                if abs(cosine) > 1e-9:
                    total = total + spec[q, 0:width, 0:128] * cosine
                if abs(sine) > 1e-9:
                    total = total - spec[q, 0:width, 128:256] * sine
            whole[slot, a] = total
        for step in range(1, parts):
            target = lax.rem(me + step, parts)
            remote(
                whole.at[slot, target], out.at[:, base + r, :], back_send.at[slot, step],
                back_recv.at[r], {"lon": target},
            ).start()
        pltpu.make_async_copy(whole.at[slot, me], out.at[:, base + r, :], back_recv.at[r]).start()

    @pl.when(is_polar)
    def _():
        @pl.loop(0, polar)
        def _(t):
            r = lax.rem(me + t, polar)
            j = base + r
            advance_row(f1, f0, j, from_west1, from_east1)

            @pl.when(owner_of(r) == me)
            def _():
                go_local(r, j).start()

            @pl.when(owner_of(r) != me)
            def _():
                go_copy(r, j).start()

        wait_z1()
        rest = jnp.where(lat == 0, polar, 0)

        @pl.loop(0, rows - polar)
        def _(t):
            advance_row(f1, f0, rest + t, from_west1, from_east1)
            keep_row(rest + t).start()

        for load in table_loads:
            load.wait()
        filter_slot(0, me)

        @pl.loop(parts, polar)
        def _(r):
            @pl.when(owner_of(r) == me)
            def _():
                filter_slot(1, r)

        @pl.loop(0, rows - polar)
        def _(t):
            keep_row(rest + t).wait()

        @pl.loop(0, polar)
        def _(r):
            slot = r // parts

            @pl.when(owner_of(r) != me)
            def _():
                go_copy(r, base + r).wait_send()
                remote(
                    whole.at[slot, me], out.at[:, base + r, :], back_send.at[slot, 0],
                    back_recv.at[r], {"lon": east},
                ).wait_recv()

            @pl.when(owner_of(r) == me)
            def _():
                for step in range(1, parts):
                    target = lax.rem(me + step, parts)
                    remote(
                        whole.at[slot, target], out.at[:, base + r, :], back_send.at[slot, step],
                        back_recv.at[r], {"lon": target},
                    ).wait_send()
                pltpu.make_async_copy(
                    whole.at[slot, me], out.at[:, base + r, :], back_recv.at[r]
                ).wait()

    @pl.when(jnp.logical_not(is_polar))
    def _():
        wait_z1()

        @pl.loop(0, rows)
        def _(t):
            advance_row(f1, f0, t, from_west1, from_east1)
            keep_row(t).start()

        for load in table_loads:
            load.wait()

        @pl.loop(0, rows)
        def _(t):
            keep_row(t).wait()

    for copy in edges0 + [east1, west1]:
        copy.wait_send()

    @pl.when(has_north)
    def _():
        up0.wait_send()
        up1.wait_send()

    @pl.when(has_south)
    def _():
        for copy in down0:
            copy.wait_send()
        down1.wait_send()


def on_block(mesh, polar, tracer, east_courant, east_diffusion, south_courant, south_diffusion, cutoff):
    rows, width, levels = tracer.shape
    parts, bands = mesh.shape["lon"], mesh.shape["lat"]
    tall, half = padded(width), parts // 2 + 1
    stack, twist = tables(parts, width)
    hbm = pl.BlockSpec(memory_space=pl.ANY)
    field = lambda count: pltpu.VMEM((count, width, levels), jnp.float32)
    edge = pltpu.VMEM((rows, levels), jnp.float32)
    edge3 = pltpu.VMEM((3, rows, levels), jnp.float32)
    slots = -(-polar // parts)
    dma = lambda *shape: pltpu.SemaphoreType.DMA(shape)
    swapped = lambda values: jnp.transpose(values, (1, 0, 2))
    result = pl.pallas_call(
        functools.partial(block_kernel, rows, width, parts, bands, polar),
        out_shape=jax.ShapeDtypeStruct((width, rows, levels), jnp.float32),
        in_specs=[pl.BlockSpec(memory_space=pltpu.SMEM)] + [hbm] * 7,
        out_specs=hbm,
        scratch_shapes=[
            field(rows + 2), field(rows + 2), field(rows), field(rows), field(rows + 1), field(rows + 1),
            pltpu.VMEM(stack.shape, jnp.bfloat16),
            pltpu.VMEM(twist.shape, jnp.float32),
            pltpu.VMEM((slots, parts, width, levels), jnp.float32),
            pltpu.VMEM((half, tall, 2 * levels), jnp.float32),
            edge, edge, edge3, edge, edge, edge,
            dma(5, rows), dma(2), dma(6), dma(6), dma(6), dma(6), dma(polar), dma(slots, parts),
            dma(slots, parts), dma(polar), dma(rows),
        ],
        compiler_params=pltpu.CompilerParams(
            collective_id=0, has_side_effects=True, vmem_limit_bytes=60 * 2**20
        ),
    )(
        cutoff, swapped(tracer), swapped(east_courant), swapped(east_diffusion),
        swapped(south_courant), swapped(south_diffusion), jnp.asarray(stack), jnp.asarray(twist),
    )
    return swapped(result)


def solution(mesh):
    in_specs = (P("lat", "lon", None),) * 5 + (P(),)
    out_specs = P("lat", "lon", None)
    parts, bands = mesh.shape["lon"], mesh.shape["lat"]

    def run(tracer, *others):
        polar = tracer.shape[0] // 6
        rows = tracer.shape[0] // bands
        fits = (
            bands > 2
            and polar + SUBSTEPS <= rows
            and parts <= polar <= parts + 2
            and parts % 8 == 0
            and tracer.shape[2] == 128
        )
        body = functools.partial(on_block, mesh, polar) if fits else on_device
        return jax.shard_map(
            body, mesh=mesh, in_specs=in_specs, out_specs=out_specs, check_vma=False
        )(tracer, *others)

    return run
```

```python
import functools
import math

import jax
import jax.numpy as jnp
import ml_dtypes
import numpy as np
from jax import lax
from jax.experimental import pallas as pl
from jax.experimental.pallas import tpu as pltpu
from jax.sharding import PartitionSpec as P

SUBSTEPS = 2


def extended(block, sides, width, periodic):
    for axis, dim in sides:
        count = lax.axis_size(axis)
        forward = [(i, i + 1) for i in range(count - 1)]
        if periodic:
            forward.append((count - 1, 0))
        backward = [(target, source) for source, target in forward]
        low = lax.ppermute(
            lax.slice_in_dim(block, block.shape[dim] - width, None, axis=dim), axis, forward
        )
        high = lax.ppermute(lax.slice_in_dim(block, 0, width, axis=dim), axis, backward)
        block = jnp.concatenate([low, block, high], axis=dim)
    return block


def advance(field, east_speed, east_mix, south_speed, south_mix):
    east_flux = east_speed[:, :-1] * 0.5 * (field[:, :-1] + field[:, 1:]) - east_mix[:, :-1] * (
        field[:, 1:] - field[:, :-1]
    )
    south_flux = south_speed[1:] * 0.5 * (field[:-1] + field[1:]) - south_mix[1:] * (
        field[1:] - field[:-1]
    )
    across = east_flux[1:-1, 1:] - east_flux[1:-1, :-1]
    meridian = south_flux[1:, 1:-1] - south_flux[:-1, 1:-1]
    return field[1:-1, 1:-1] - across - meridian


def split_four(coefs, levels):
    return (
        coefs[:, :, :levels],
        coefs[:, :, levels : 2 * levels],
        coefs[:, :, 2 * levels : 3 * levels],
        coefs[:, :, 3 * levels :],
    )


def extend(values, depth):
    beside_all = extended(values, (("lon", 1),), depth, True)
    return extended(beside_all, (("lat", 0),), depth, False)


def angles(rows, cols, length):
    first = jnp.arange(rows, dtype=jnp.int32)
    second = jnp.arange(cols, dtype=jnp.int32)
    phase = first[:, None] * second[None, :] % length
    angle = phase.astype(jnp.float32) * (2.0 * math.pi / length)
    return (jnp.cos(angle), jnp.sin(angle))


def contract(form, values, table):
    return jnp.einsum(
        form, values, table, precision=lax.Precision.HIGHEST, preferred_element_type=jnp.float32
    )


def rotate(real, imag, cosine, sine, form, sign):
    new_real = contract(form, real, cosine) - sign * contract(form, imag, sine)
    new_imag = contract(form, imag, cosine) + sign * contract(form, real, sine)
    return (new_real, new_imag)


def pick_factor(length):
    factor = 1
    for candidate in range(1, int(math.isqrt(length)) + 1):
        if length % candidate == 0:
            factor = candidate
    return factor


def filter_rows_local(whole_rows, item_cut):
    share, length, levels = whole_rows.shape
    outer = pick_factor(length)
    inner = length // outer
    shaped = whole_rows.reshape(share, outer, inner, levels)
    cos_outer, sin_outer = angles(outer, outer, outer)
    cos_inner, sin_inner = angles(inner, inner, inner)
    cos_twist, sin_twist = angles(outer, inner, length)
    first_real = contract("janl,ak->jknl", shaped, cos_outer)
    first_imag = -contract("janl,ak->jknl", shaped, sin_outer)
    twist_real = cos_twist[None, :, :, None]
    twist_imag = sin_twist[None, :, :, None]
    turned_real = first_real * twist_real + first_imag * twist_imag
    turned_imag = first_imag * twist_real - first_real * twist_imag
    spec_real, spec_imag = rotate(
        turned_real, turned_imag, cos_inner, sin_inner, "jknl,nm->jkml", -1.0
    )
    low = jnp.arange(outer, dtype=jnp.int32)
    high = jnp.arange(inner, dtype=jnp.int32)
    wave = low[:, None] + outer * high[None, :]
    folded = jnp.minimum(wave, length - wave).astype(jnp.float32)
    levelled = item_cut.astype(jnp.float32)[:, None, None]
    damping = jnp.minimum(1.0, (levelled / jnp.maximum(folded, 1.0)[None, :, :]) ** 2) / length
    spec_real = spec_real * damping[:, :, :, None]
    spec_imag = spec_imag * damping[:, :, :, None]
    back_real, back_imag = rotate(spec_real, spec_imag, cos_inner, sin_inner, "jkml,nm->jknl", 1.0)
    unturned_real = back_real * twist_real - back_imag * twist_imag
    unturned_imag = back_imag * twist_real + back_real * twist_imag
    result = contract("jknl,ak->janl", unturned_real, cos_outer) - contract(
        "jknl,ak->janl", unturned_imag, sin_outer
    )
    return result.reshape(share, length, levels)


def smooth_rows(block, global_rows, cutoff):
    whole_rows = lax.all_to_all(block, "lon", split_axis=0, concat_axis=1, tiled=True)
    share = whole_rows.shape[0]
    length = whole_rows.shape[1]
    first = lax.axis_index("lon") * share
    item_row = lax.dynamic_slice_in_dim(global_rows, first, share, 0)
    matcher = item_row[:, None] == jnp.arange(cutoff.shape[0], dtype=jnp.int32)[None, :]
    item_cut = jnp.sum(jnp.where(matcher, cutoff[None, :], 0), axis=1)
    smoothed = filter_rows_local(whole_rows, item_cut)
    kept = jnp.where((item_cut < length // 2)[:, None, None], smoothed, whole_rows)
    return lax.all_to_all(kept, "lon", split_axis=1, concat_axis=0, tiled=True)


def on_device(tracer, east_courant, east_diffusion, south_courant, south_diffusion, cutoff):
    count, width, levels = tracer.shape
    lat_pos = lax.axis_index("lat")
    rows_here = lat_pos * count + jnp.arange(count, dtype=jnp.int32)
    keeper = (rows_here > 0).astype(jnp.float32)[:, None, None]
    coefs = jnp.concatenate(
        [east_courant, east_diffusion, south_courant * keeper, south_diffusion * keeper], 2
    )
    field = tracer
    coef_ext = extend(coefs, 1)
    for substep in range(SUBSTEPS):
        field = advance(extend(field, 1), *split_four(coef_ext, levels))
    field = smooth_rows(field, rows_here, cutoff)
    return field


MESH = pl.DeviceIdType.MESH


def padded(length):
    return -(-length // 16) * 16


def split_bf16(values):
    high = values.astype(ml_dtypes.bfloat16)
    low = (values - high.astype(np.float64)).astype(ml_dtypes.bfloat16)
    return high, low


def tables(parts, width):
    tall = padded(width)
    place = np.arange(width)
    angle = (place[:, None] * place[None, :] % width) * (2.0 * np.pi / width)
    stack = np.zeros((4, tall, tall), ml_dtypes.bfloat16)
    cos_high, cos_low = split_bf16(np.cos(angle))
    sin_high, sin_low = split_bf16(np.sin(angle))
    for index, table in enumerate((cos_high, sin_high, cos_low, sin_low)):
        stack[index, :width, :width] = table
    half = parts // 2 + 1
    turn = np.arange(half)[:, None] * place[None, :] * (2.0 * np.pi / (parts * width))
    twist = np.zeros((2, half, tall, 128), np.float32)
    twist[0, :, :width] = np.cos(turn)[:, :, None]
    twist[1, :, :width] = np.sin(turn)[:, :, None]
    return stack.reshape(4 * tall, tall), twist


def block_kernel(
    rows, width, parts, bands, polar, kept_owner, lent_owner,
    cut_ref, f_in, ec_in, ed_in, sc_in, sd_in, dft_in, tw_in, out,
    f0, f1, ec, ed, sc, sd, dft, tw, whole, spec, lent, lent_back,
    to_east1, to_west1, from_west0, from_east0, from_west1, from_east1,
    to_east2, to_west2, from_west2, from_east2,
    load_sem, table_sem, lon_send, lon_recv, z_send, z_recv, go_send, go_recv, back_send, back_recv,
    lend_send, lend_recv, ret_send, ret_recv, out_sem,
):
    me = lax.axis_index("lon")
    lat = lax.axis_index("lat")
    east = lax.rem(me + 1, parts)
    west = lax.rem(me + parts - 1, parts)
    has_south = lat > 0
    has_north = lat < bands - 1
    is_polar = jnp.logical_or(lat == 0, lat == bands - 1)
    kept, borrowed = len(kept_owner), len(lent_owner)
    ascending = lat < bands // 2
    base = jnp.where(ascending, 0, rows - polar)
    pole_lat = jnp.where(ascending, 0, bands - 1)
    helper_lat = jnp.where(ascending, 1, bands - 2)
    early = polar + 1
    tall = padded(width)
    half = parts // 2 + 1

    def place(t):
        return jnp.where(ascending, t, rows - 1 - t)

    def load_row(j):
        return [
            pltpu.make_async_copy(src.at[:, j, :], dst.at[j + shift], load_sem.at[index, j])
            for index, (src, dst, shift) in enumerate(
                ((f_in, f0, 1), (ec_in, ec, 0), (ed_in, ed, 0), (sc_in, sc, 0), (sd_in, sd, 0))
            )
        ]

    @pl.loop(0, rows)
    def _(t):
        for load in load_row(place(t)):
            load.start()

    table_loads = [
        pltpu.make_async_copy(dft_in, dft, table_sem.at[0]),
        pltpu.make_async_copy(tw_in, tw, table_sem.at[1]),
    ]
    for load in table_loads:
        load.start()

    barrier = pltpu.get_barrier_semaphore()
    for step in range(1, parts):
        pl.semaphore_signal(
            barrier, 1, device_id={"lon": lax.rem(me + step, parts)}, device_id_type=MESH
        )

    @pl.when(has_south)
    def _():
        pl.semaphore_signal(barrier, 1, device_id={"lat": lat - 1}, device_id_type=MESH)

    @pl.when(has_north)
    def _():
        pl.semaphore_signal(barrier, 1, device_id={"lat": lat + 1}, device_id_type=MESH)

    peers = parts - 1 + jnp.where(has_south, 1, 0) + jnp.where(has_north, 1, 0)
    pl.semaphore_wait(barrier, peers)

    def remote(src, dst, send, recv, where):
        return pltpu.make_async_remote_copy(
            src_ref=src, dst_ref=dst, send_sem=send, recv_sem=recv,
            device_id=where, device_id_type=MESH,
        )

    north = {"lat": lax.rem(lat + 1, bands)}
    south = {"lat": lax.rem(lat + bands - 1, bands)}
    up0 = remote(f_in.at[:, rows - 1, :], f0.at[0], z_send.at[0], z_recv.at[0], north)
    down0 = [
        remote(f_in.at[:, 0, :], f0.at[rows + 1], z_send.at[1], z_recv.at[1], south),
        remote(sc_in.at[:, 0, :], sc.at[rows], z_send.at[2], z_recv.at[2], south),
        remote(sd_in.at[:, 0, :], sd.at[rows], z_send.at[3], z_recv.at[3], south),
    ]
    up1 = remote(f1.at[rows], f1.at[0], z_send.at[4], z_recv.at[4], north)
    down1 = remote(f1.at[1], f1.at[rows + 1], z_send.at[5], z_recv.at[5], south)
    edges0 = [
        remote(f_in.at[width - 1], from_west0.at[0], lon_send.at[0], lon_recv.at[0], {"lon": east}),
        remote(ec_in.at[width - 1], from_west0.at[1], lon_send.at[1], lon_recv.at[1], {"lon": east}),
        remote(ed_in.at[width - 1], from_west0.at[2], lon_send.at[4], lon_recv.at[4], {"lon": east}),
        remote(f_in.at[0], from_east0, lon_send.at[5], lon_recv.at[5], {"lon": west}),
    ]
    edges1 = [
        remote(to_east1, from_west1, lon_send.at[2], lon_recv.at[2], {"lon": east}),
        remote(to_west1, from_east1, lon_send.at[3], lon_recv.at[3], {"lon": west}),
    ]
    edges2 = [
        remote(to_east2, from_west2, lon_send.at[6], lon_recv.at[6], {"lon": east}),
        remote(to_west2, from_east2, lon_send.at[7], lon_recv.at[7], {"lon": west}),
    ]

    for copy in edges0:
        copy.start()

    @pl.when(has_north)
    def _():
        up0.start()

    @pl.when(has_south)
    def _():
        for copy in down0:
            copy.start()

    for load in load_row(place(0)):
        load.wait()
    nothing = jnp.zeros((width, 128), jnp.float32)

    @pl.when(lat == 0)
    def _():
        f0[0] = nothing
        f1[0] = nothing
        sc[0] = nothing
        sd[0] = nothing

    @pl.when(lat == bands - 1)
    def _():
        f0[rows + 1] = nothing
        f1[rows + 1] = nothing
        sc[rows] = nothing
        sd[rows] = nothing

    def advance_row(src, dst, j, edge, beyond):
        value = src[j + 1]
        beside = jnp.concatenate([value[1:], beyond], axis=0)
        flux = ec[j] * 0.5 * (value + beside) - ed[j] * (beside - value)
        first = value[0:1]
        entering = from_west0[1, pl.ds(j, 1), :] * 0.5 * (edge + first) - from_west0[2, pl.ds(j, 1), :] * (first - edge)
        flux_west = jnp.concatenate([entering, flux[:-1]], axis=0)
        below = src[j]
        above = src[j + 2]
        flux_south = sc[j] * 0.5 * (below + value) - sd[j] * (value - below)
        flux_north = sc[j + 1] * 0.5 * (value + above) - sd[j + 1] * (above - value)
        dst[j + 1] = value - (flux - flux_west) - (flux_north - flux_south)

    def wait_z0():
        @pl.when(has_south)
        def _():
            up0.wait_recv()

        @pl.when(has_north)
        def _():
            for copy in down0:
                copy.wait_recv()

    def wait_z1(from_south):
        @pl.when(from_south)
        def _():
            up1.wait_recv()

        @pl.when(jnp.logical_not(from_south))
        def _():
            down1.wait_recv()

    @pl.when(jnp.logical_not(is_polar))
    def _():
        wait_z0()

    for copy in edges0:
        copy.wait_recv()

    def first_substep(start, stop, east_edge, west_edge):
        @pl.loop(start, stop)
        def _(t):
            j = place(t)

            @pl.when(t < rows - 1)
            def _():
                for load in load_row(place(t + 1)):
                    load.wait()

            advance_row(f0, f1, j, from_west0[0, pl.ds(j, 1), :], from_east0[pl.ds(j, 1), :])
            east_edge[pl.ds(t - start, 1), :] = f1[j + 1, width - 1 : width, :]
            west_edge[pl.ds(t - start, 1), :] = f1[j + 1, 0:1, :]

    def finish_first():
        first_substep(early, rows, to_east2, to_west2)
        for copy in edges2:
            copy.start()

        @pl.when(has_north)
        def _():
            up1.start()

        @pl.when(has_south)
        def _():
            down1.start()

    def second_early(t):
        advance_row(f1, f0, place(t), from_west1[pl.ds(t, 1), :], from_east1[pl.ds(t, 1), :])

    def second_late(t):
        late = t - early
        advance_row(f1, f0, place(t), from_west2[pl.ds(late, 1), :], from_east2[pl.ds(late, 1), :])

    first_substep(0, early, to_east1, to_west1)
    for copy in edges1:
        copy.start()

    def keep_row(j):
        return pltpu.make_async_copy(f0.at[j + 1], out.at[:, j, :], out_sem.at[j])

    def pick(table, index):
        value = table[0]
        for position in range(1, len(table)):
            value = jnp.where(index == position, table[position], value)
        return value

    def send_piece(src, index, owner):
        @pl.when(owner == me)
        def _():
            pltpu.make_async_copy(src, whole.at[me], go_send.at[index]).start()

        @pl.when(owner != me)
        def _():
            remote(src, whole.at[me], go_send.at[index], go_recv.at[me], {"lon": owner}).start()

    def filter_row(r):
        for step in range(1, parts):
            source = lax.rem(me + step, parts)
            remote(
                f0.at[1], whole.at[source], go_send.at[0], go_recv.at[source], {"lon": source}
            ).wait_recv()
        extra = jnp.zeros((tall - width, 128), jnp.float32)
        pieces = [whole[a] for a in range(parts)]
        for q in range(half):
            real, imag = None, None
            for a in range(parts // 2):
                merged = (
                    pieces[a] + pieces[a + parts // 2] if q % 2 == 0 else pieces[a] - pieces[a + parts // 2]
                )
                turn = 2.0 * math.pi * ((a * q) % parts) / parts
                cosine, sine = math.cos(turn), math.sin(turn)
                if abs(cosine) > 1e-9:
                    term = merged if cosine > 1 - 1e-9 else merged * cosine
                    real = term if real is None else real + term
                if abs(sine) > 1e-9:
                    term = merged * (-sine)
                    imag = term if imag is None else imag + term
            real = jnp.concatenate([real, extra], axis=0)
            if imag is None:
                new_real = real * tw[0, q]
                new_imag = -real * tw[1, q]
            else:
                imag = jnp.concatenate([imag, extra], axis=0)
                new_real = real * tw[0, q] + imag * tw[1, q]
                new_imag = imag * tw[0, q] - real * tw[1, q]
            spec[q, :, 0:128] = new_real
            spec[q, :, 128:256] = new_imag

        cut = cut_ref[pole_lat * rows + base + r].astype(jnp.float32)
        length = parts * width

        def products(values):
            high = values.astype(jnp.bfloat16)
            low = (values - high.astype(jnp.float32)).astype(jnp.bfloat16)
            main = jnp.dot(dft[...], high, preferred_element_type=jnp.float32)
            rest = jnp.dot(dft[0 : 2 * tall, :], low, preferred_element_type=jnp.float32)
            by_cos = main[0:tall] + (main[2 * tall : 3 * tall] + rest[0:tall])
            by_sin = main[tall : 2 * tall] + (main[3 * tall : 4 * tall] + rest[tall : 2 * tall])
            return by_cos, by_sin

        @pl.loop(0, half)
        def _(q):
            by_cos, by_sin = products(spec[q])
            real = by_cos[:, 0:128] + by_sin[:, 128:256]
            imag = by_cos[:, 128:256] - by_sin[:, 0:128]
            wave = q + parts * lax.broadcasted_iota(jnp.int32, (tall, 128), 0)
            folded = jnp.maximum(jnp.minimum(wave, length - wave), 1).astype(jnp.float32)
            ratio = cut / folded
            damping = jnp.minimum(1.0, ratio * ratio) * (1.0 / length)
            both = jnp.concatenate([real * damping, imag * damping], axis=1)
            by_cos, by_sin = products(both)
            real = by_cos[:, 0:128] - by_sin[:, 128:256]
            imag = by_cos[:, 128:256] + by_sin[:, 0:128]
            spec[q, :, 0:128] = real * tw[0, q] - imag * tw[1, q]
            spec[q, :, 128:256] = imag * tw[0, q] + real * tw[1, q]

        for a in range(parts):
            total = spec[0, 0:width, 0:128]
            for q in range(1, half):
                turn = 2.0 * math.pi * ((a * q) % parts) / parts
                weight = 1.0 if q == parts // 2 else 2.0
                cosine, sine = weight * math.cos(turn), weight * math.sin(turn)
                if abs(cosine) > 1e-9:
                    total = total + spec[q, 0:width, 0:128] * cosine
                if abs(sine) > 1e-9:
                    total = total - spec[q, 0:width, 128:256] * sine
            whole[a] = total

    def run_owner(owners, index_of, row_of, landing):
        for index, owner in enumerate(owners):
            @pl.when(owner == me)
            def _():
                pltpu.make_async_copy(f0.at[1], whole.at[me], go_send.at[index]).wait()

        owned = functools.reduce(jnp.logical_or, [owner == me for owner in owners])

        @pl.when(owned)
        def _():
            index = index_of(me)
            filter_row(row_of(index))
            for step in range(1, parts):
                target = lax.rem(me + step, parts)
                remote(
                    whole.at[target], landing(index), back_send.at[step], back_recv.at[index],
                    {"lon": target},
                ).start()
            pltpu.make_async_copy(whole.at[me], landing(index), back_recv.at[index]).start()

    def finish_owner(owners, landing):
        owned = functools.reduce(jnp.logical_or, [owner == me for owner in owners])

        @pl.when(owned)
        def _():
            for step in range(1, parts):
                target = lax.rem(me + step, parts)
                remote(
                    whole.at[target], landing(0), back_send.at[step], back_recv.at[0],
                    {"lon": target},
                ).wait_send()

    def wait_back(index, owner, landing):
        @pl.when(owner == me)
        def _():
            pltpu.make_async_copy(whole.at[me], landing(index), back_recv.at[index]).wait()

        @pl.when(owner != me)
        def _():
            remote(
                whole.at[me], landing(index), back_send.at[0], back_recv.at[index], {"lon": east}
            ).wait_recv()

    def wait_sent(index, owner, src):
        @pl.when(owner != me)
        def _():
            remote(src, whole.at[me], go_send.at[index], go_recv.at[me], {"lon": owner}).wait_send()

    def inverse(owners):
        table = [owners.index(device) if device in owners else 0 for device in range(parts)]
        return functools.partial(pick, table)

    def lend(m):
        j = base + kept + m
        return remote(f0.at[j + 1], lent.at[m], lend_send.at[m], lend_recv.at[m], {"lat": helper_lat})

    def give_back(m):
        return remote(
            lent_back.at[m], out.at[:, base + kept + m, :], ret_send.at[m], ret_recv.at[m],
            {"lat": pole_lat},
        )

    def kept_landing(r):
        return out.at[:, base + r, :]

    def lent_landing(m):
        return lent_back.at[m]

    @pl.when(is_polar)
    def _():
        for copy in edges1:
            copy.wait_recv()

        @pl.loop(0, polar)
        def _(step):
            r = jnp.where(step < borrowed, kept + step, lax.rem(me + step - borrowed, kept))
            second_early(place(base + r))

            @pl.when(step < borrowed)
            def _():
                lend(step).start()

            @pl.when(step >= borrowed)
            def _():
                send_piece(f0.at[base + r + 1], r, pick(kept_owner, r))

        wait_z0()
        finish_first()
        second_early(polar)
        keep_row(place(polar)).start()
        wait_z1(lat > 0)
        for copy in edges2:
            copy.wait_recv()

        @pl.loop(early, rows)
        def _(t):
            second_late(t)
            keep_row(place(t)).start()

        for load in table_loads:
            load.wait()
        run_owner(kept_owner, inverse(kept_owner), lambda r: r, kept_landing)

        @pl.loop(polar, rows)
        def _(t):
            keep_row(place(t)).wait()

        @pl.loop(0, kept)
        def _(r):
            wait_sent(r, pick(kept_owner, r), f0.at[1])
            wait_back(r, pick(kept_owner, r), kept_landing)

        finish_owner(kept_owner, kept_landing)

        @pl.loop(0, borrowed)
        def _(m):
            lend(m).wait_send()
            give_back(m).wait_recv()

    @pl.when(jnp.logical_not(is_polar))
    def _():
        finish_first()
        for copy in edges1 + edges2:
            copy.wait_recv()
        wait_z1(jnp.logical_not(ascending))

        @pl.loop(0, rows - 1)
        def _(step):
            t = rows - 1 - step

            @pl.when(t >= early)
            def _():
                second_late(t)

            @pl.when(t < early)
            def _():
                second_early(t)

            keep_row(place(t)).start()
            for m in range(borrowed):
                @pl.when(step == 5 + 3 * m)
                def _():
                    lend(m).wait_recv()
                    send_piece(lent.at[m], m, lent_owner[m])

        wait_z1(ascending)
        second_early(0)
        keep_row(place(0)).start()
        for load in table_loads:
            load.wait()
        run_owner(lent_owner, inverse(lent_owner), lambda m: kept + m, lent_landing)

        @pl.loop(0, borrowed)
        def _(m):
            wait_back(m, pick(lent_owner, m), lent_landing)
            give_back(m).start()

        @pl.loop(0, rows)
        def _(t):
            keep_row(t).wait()

        @pl.loop(0, borrowed)
        def _(m):
            wait_sent(m, pick(lent_owner, m), lent.at[m])
            give_back(m).wait_send()

        finish_owner(lent_owner, lent_landing)

    for copy in edges0 + edges1 + edges2:
        copy.wait_send()

    @pl.when(has_north)
    def _():
        up0.wait_send()
        up1.wait_send()

    @pl.when(has_south)
    def _():
        for copy in down0:
            copy.wait_send()
        down1.wait_send()


def share_rows(polar):
    lent = 2 * polar // 5
    return (0, 7, 2, 4, 1, 6, 3, 5)[: polar - lent], (0, 2, 4, 6, 1, 3, 5, 7)[:lent]


def on_block(mesh, polar, tracer, east_courant, east_diffusion, south_courant, south_diffusion, cutoff):
    rows, width, levels = tracer.shape
    parts, bands = mesh.shape["lon"], mesh.shape["lat"]
    tall, half = padded(width), parts // 2 + 1
    stack, twist = tables(parts, width)
    hbm = pl.BlockSpec(memory_space=pl.ANY)
    field = lambda count: pltpu.VMEM((count, width, levels), jnp.float32)
    edge = pltpu.VMEM((rows, levels), jnp.float32)
    edge3 = pltpu.VMEM((3, rows, levels), jnp.float32)
    kept_owner, lent_owner = share_rows(polar)
    late = pltpu.VMEM((padded(rows - polar), levels), jnp.float32)
    most = max(len(kept_owner), len(lent_owner))
    some = len(lent_owner)
    dma = lambda *shape: pltpu.SemaphoreType.DMA(shape)
    swapped = lambda values: jnp.transpose(values, (1, 0, 2))
    result = pl.pallas_call(
        functools.partial(block_kernel, rows, width, parts, bands, polar, kept_owner, lent_owner),
        out_shape=jax.ShapeDtypeStruct((width, rows, levels), jnp.float32),
        in_specs=[pl.BlockSpec(memory_space=pltpu.SMEM)] + [hbm] * 7,
        out_specs=hbm,
        scratch_shapes=[
            field(rows + 2), field(rows + 2), field(rows), field(rows), field(rows + 1), field(rows + 1),
            pltpu.VMEM(stack.shape, jnp.bfloat16),
            pltpu.VMEM(twist.shape, jnp.float32),
            field(parts),
            pltpu.VMEM((half, tall, 2 * levels), jnp.float32),
            field(some), field(some),
            edge, edge, edge3, edge, edge, edge, late, late, late, late,
            dma(5, rows), dma(2), dma(8), dma(8), dma(6), dma(6), dma(most), dma(parts),
            dma(parts), dma(most), dma(some), dma(some), dma(some), dma(some), dma(rows),
        ],
        compiler_params=pltpu.CompilerParams(
            collective_id=0, has_side_effects=True, vmem_limit_bytes=60 * 2**20
        ),
    )(
        cutoff, swapped(tracer), swapped(east_courant), swapped(east_diffusion),
        swapped(south_courant), swapped(south_diffusion), jnp.asarray(stack), jnp.asarray(twist),
    )
    return swapped(result)


def solution(mesh):
    in_specs = (P("lat", "lon", None),) * 5 + (P(),)
    out_specs = P("lat", "lon", None)
    parts, bands = mesh.shape["lon"], mesh.shape["lat"]

    def run(tracer, *others):
        polar = tracer.shape[0] // 6
        rows = tracer.shape[0] // bands
        fits = (
            bands == 4
            and polar + SUBSTEPS < rows
            and 5 <= polar <= 13
            and parts == 8
            and tracer.shape[2] == 128
        )
        body = functools.partial(on_block, mesh, polar) if fits else on_device
        return jax.shard_map(
            body, mesh=mesh, in_specs=in_specs, out_specs=out_specs, check_vma=False
        )(tracer, *others)

    return run
```

```python
import functools
import math

import jax
import jax.numpy as jnp
import ml_dtypes
import numpy as np
from jax import lax
from jax.experimental import pallas as pl
from jax.experimental.pallas import tpu as pltpu
from jax.sharding import PartitionSpec as P

SUBSTEPS = 2


def extended(block, sides, width, periodic):
    for axis, dim in sides:
        count = lax.axis_size(axis)
        forward = [(i, i + 1) for i in range(count - 1)]
        if periodic:
            forward.append((count - 1, 0))
        backward = [(target, source) for source, target in forward]
        low = lax.ppermute(
            lax.slice_in_dim(block, block.shape[dim] - width, None, axis=dim), axis, forward
        )
        high = lax.ppermute(lax.slice_in_dim(block, 0, width, axis=dim), axis, backward)
        block = jnp.concatenate([low, block, high], axis=dim)
    return block


def advance(field, east_speed, east_mix, south_speed, south_mix):
    east_flux = east_speed[:, :-1] * 0.5 * (field[:, :-1] + field[:, 1:]) - east_mix[:, :-1] * (
        field[:, 1:] - field[:, :-1]
    )
    south_flux = south_speed[1:] * 0.5 * (field[:-1] + field[1:]) - south_mix[1:] * (
        field[1:] - field[:-1]
    )
    across = east_flux[1:-1, 1:] - east_flux[1:-1, :-1]
    meridian = south_flux[1:, 1:-1] - south_flux[:-1, 1:-1]
    return field[1:-1, 1:-1] - across - meridian


def split_four(coefs, levels):
    return (
        coefs[:, :, :levels],
        coefs[:, :, levels : 2 * levels],
        coefs[:, :, 2 * levels : 3 * levels],
        coefs[:, :, 3 * levels :],
    )


def extend(values, depth):
    beside_all = extended(values, (("lon", 1),), depth, True)
    return extended(beside_all, (("lat", 0),), depth, False)


def angles(rows, cols, length):
    first = jnp.arange(rows, dtype=jnp.int32)
    second = jnp.arange(cols, dtype=jnp.int32)
    phase = first[:, None] * second[None, :] % length
    angle = phase.astype(jnp.float32) * (2.0 * math.pi / length)
    return (jnp.cos(angle), jnp.sin(angle))


def contract(form, values, table):
    return jnp.einsum(
        form, values, table, precision=lax.Precision.HIGHEST, preferred_element_type=jnp.float32
    )


def rotate(real, imag, cosine, sine, form, sign):
    new_real = contract(form, real, cosine) - sign * contract(form, imag, sine)
    new_imag = contract(form, imag, cosine) + sign * contract(form, real, sine)
    return (new_real, new_imag)


def pick_factor(length):
    factor = 1
    for candidate in range(1, int(math.isqrt(length)) + 1):
        if length % candidate == 0:
            factor = candidate
    return factor


def filter_rows_local(whole_rows, item_cut):
    share, length, levels = whole_rows.shape
    outer = pick_factor(length)
    inner = length // outer
    shaped = whole_rows.reshape(share, outer, inner, levels)
    cos_outer, sin_outer = angles(outer, outer, outer)
    cos_inner, sin_inner = angles(inner, inner, inner)
    cos_twist, sin_twist = angles(outer, inner, length)
    first_real = contract("janl,ak->jknl", shaped, cos_outer)
    first_imag = -contract("janl,ak->jknl", shaped, sin_outer)
    twist_real = cos_twist[None, :, :, None]
    twist_imag = sin_twist[None, :, :, None]
    turned_real = first_real * twist_real + first_imag * twist_imag
    turned_imag = first_imag * twist_real - first_real * twist_imag
    spec_real, spec_imag = rotate(
        turned_real, turned_imag, cos_inner, sin_inner, "jknl,nm->jkml", -1.0
    )
    low = jnp.arange(outer, dtype=jnp.int32)
    high = jnp.arange(inner, dtype=jnp.int32)
    wave = low[:, None] + outer * high[None, :]
    folded = jnp.minimum(wave, length - wave).astype(jnp.float32)
    levelled = item_cut.astype(jnp.float32)[:, None, None]
    damping = jnp.minimum(1.0, (levelled / jnp.maximum(folded, 1.0)[None, :, :]) ** 2) / length
    spec_real = spec_real * damping[:, :, :, None]
    spec_imag = spec_imag * damping[:, :, :, None]
    back_real, back_imag = rotate(spec_real, spec_imag, cos_inner, sin_inner, "jkml,nm->jknl", 1.0)
    unturned_real = back_real * twist_real - back_imag * twist_imag
    unturned_imag = back_imag * twist_real + back_real * twist_imag
    result = contract("jknl,ak->janl", unturned_real, cos_outer) - contract(
        "jknl,ak->janl", unturned_imag, sin_outer
    )
    return result.reshape(share, length, levels)


def smooth_rows(block, global_rows, cutoff):
    whole_rows = lax.all_to_all(block, "lon", split_axis=0, concat_axis=1, tiled=True)
    share = whole_rows.shape[0]
    length = whole_rows.shape[1]
    first = lax.axis_index("lon") * share
    item_row = lax.dynamic_slice_in_dim(global_rows, first, share, 0)
    matcher = item_row[:, None] == jnp.arange(cutoff.shape[0], dtype=jnp.int32)[None, :]
    item_cut = jnp.sum(jnp.where(matcher, cutoff[None, :], 0), axis=1)
    smoothed = filter_rows_local(whole_rows, item_cut)
    kept = jnp.where((item_cut < length // 2)[:, None, None], smoothed, whole_rows)
    return lax.all_to_all(kept, "lon", split_axis=1, concat_axis=0, tiled=True)


def on_device(tracer, east_courant, east_diffusion, south_courant, south_diffusion, cutoff):
    count, width, levels = tracer.shape
    lat_pos = lax.axis_index("lat")
    rows_here = lat_pos * count + jnp.arange(count, dtype=jnp.int32)
    keeper = (rows_here > 0).astype(jnp.float32)[:, None, None]
    coefs = jnp.concatenate(
        [east_courant, east_diffusion, south_courant * keeper, south_diffusion * keeper], 2
    )
    field = tracer
    coef_ext = extend(coefs, 1)
    for substep in range(SUBSTEPS):
        field = advance(extend(field, 1), *split_four(coef_ext, levels))
    field = smooth_rows(field, rows_here, cutoff)
    return field


MESH = pl.DeviceIdType.MESH


def padded(length):
    return -(-length // 16) * 16


def split_bf16(values):
    high = values.astype(ml_dtypes.bfloat16)
    low = (values - high.astype(np.float64)).astype(ml_dtypes.bfloat16)
    return high, low


def tables(parts, width):
    tall = padded(width)
    place = np.arange(width)
    angle = (place[:, None] * place[None, :] % width) * (2.0 * np.pi / width)
    stack = np.zeros((4, tall, tall), ml_dtypes.bfloat16)
    cos_high, cos_low = split_bf16(np.cos(angle))
    sin_high, sin_low = split_bf16(np.sin(angle))
    for index, table in enumerate((cos_high, sin_high, cos_low, sin_low)):
        stack[index, :width, :width] = table
    half = parts // 2 + 1
    turn = np.arange(half)[:, None] * place[None, :] * (2.0 * np.pi / (parts * width))
    twist = np.zeros((2, half, tall, 128), np.float32)
    twist[0, :, :width] = np.cos(turn)[:, :, None]
    twist[1, :, :width] = np.sin(turn)[:, :, None]
    return stack.reshape(4 * tall, tall), twist


def block_kernel(
    rows, width, parts, bands, polar, kept_owner, lent_owner,
    cut_ref, f_in, ec_in, ed_in, sc_in, sd_in, dft_in, tw_in, out,
    f0, f1, ec, ed, sc, sd, dft, tw, whole, spec, lent, lent_back, land,
    to_east1, to_west1, from_west0, from_east0, from_west1, from_east1,
    to_east2, to_west2, from_west2, from_east2,
    load_sem, table_sem, lon_send, lon_recv, z_send, z_recv, go_send, go_recv, back_send, back_recv,
    lend_send, lend_recv, ret_send, ret_recv, out_sem,
):
    me = lax.axis_index("lon")
    lat = lax.axis_index("lat")
    east = lax.rem(me + 1, parts)
    west = lax.rem(me + parts - 1, parts)
    has_south = lat > 0
    has_north = lat < bands - 1
    is_polar = jnp.logical_or(lat == 0, lat == bands - 1)
    kept, borrowed = len(kept_owner), len(lent_owner)
    ascending = lat < bands // 2
    base = jnp.where(ascending, 0, rows - polar)
    pole_lat = jnp.where(ascending, 0, bands - 1)
    helper_lat = jnp.where(ascending, 1, bands - 2)
    early = polar + 1
    fold, sub = 2 * parts, width // 2
    tall = padded(sub)
    half = fold // 2 + 1

    def place(t):
        return jnp.where(ascending, t, rows - 1 - t)

    def load_row(j):
        return [
            pltpu.make_async_copy(src.at[:, j, :], dst.at[j + shift], load_sem.at[index, j])
            for index, (src, dst, shift) in enumerate(
                ((f_in, f0, 1), (ec_in, ec, 0), (ed_in, ed, 0), (sc_in, sc, 0), (sd_in, sd, 0))
            )
        ]

    @pl.loop(0, rows)
    def _(t):
        for load in load_row(place(t)):
            load.start()

    table_loads = [
        pltpu.make_async_copy(dft_in, dft, table_sem.at[0]),
        pltpu.make_async_copy(tw_in, tw, table_sem.at[1]),
    ]
    for load in table_loads:
        load.start()

    barrier = pltpu.get_barrier_semaphore()
    for step in range(1, parts):
        pl.semaphore_signal(
            barrier, 1, device_id={"lon": lax.rem(me + step, parts)}, device_id_type=MESH
        )

    @pl.when(has_south)
    def _():
        pl.semaphore_signal(barrier, 1, device_id={"lat": lat - 1}, device_id_type=MESH)

    @pl.when(has_north)
    def _():
        pl.semaphore_signal(barrier, 1, device_id={"lat": lat + 1}, device_id_type=MESH)

    peers = parts - 1 + jnp.where(has_south, 1, 0) + jnp.where(has_north, 1, 0)
    pl.semaphore_wait(barrier, peers)

    def remote(src, dst, send, recv, where):
        return pltpu.make_async_remote_copy(
            src_ref=src, dst_ref=dst, send_sem=send, recv_sem=recv,
            device_id=where, device_id_type=MESH,
        )

    north = {"lat": lax.rem(lat + 1, bands)}
    south = {"lat": lax.rem(lat + bands - 1, bands)}
    up0 = remote(f_in.at[:, rows - 1, :], f0.at[0], z_send.at[0], z_recv.at[0], north)
    down0 = [
        remote(f_in.at[:, 0, :], f0.at[rows + 1], z_send.at[1], z_recv.at[1], south),
        remote(sc_in.at[:, 0, :], sc.at[rows], z_send.at[2], z_recv.at[2], south),
        remote(sd_in.at[:, 0, :], sd.at[rows], z_send.at[3], z_recv.at[3], south),
    ]
    up1 = remote(f1.at[rows], f1.at[0], z_send.at[4], z_recv.at[4], north)
    down1 = remote(f1.at[1], f1.at[rows + 1], z_send.at[5], z_recv.at[5], south)
    edges0 = [
        remote(f_in.at[width - 1], from_west0.at[0], lon_send.at[0], lon_recv.at[0], {"lon": east}),
        remote(ec_in.at[width - 1], from_west0.at[1], lon_send.at[1], lon_recv.at[1], {"lon": east}),
        remote(ed_in.at[width - 1], from_west0.at[2], lon_send.at[4], lon_recv.at[4], {"lon": east}),
        remote(f_in.at[0], from_east0, lon_send.at[5], lon_recv.at[5], {"lon": west}),
    ]
    edges1 = [
        remote(to_east1, from_west1, lon_send.at[2], lon_recv.at[2], {"lon": east}),
        remote(to_west1, from_east1, lon_send.at[3], lon_recv.at[3], {"lon": west}),
    ]
    edges2 = [
        remote(to_east2, from_west2, lon_send.at[6], lon_recv.at[6], {"lon": east}),
        remote(to_west2, from_east2, lon_send.at[7], lon_recv.at[7], {"lon": west}),
    ]

    for copy in edges0:
        copy.start()

    @pl.when(has_north)
    def _():
        up0.start()

    @pl.when(has_south)
    def _():
        for copy in down0:
            copy.start()

    for load in load_row(place(0)):
        load.wait()
    nothing = jnp.zeros((width, 128), jnp.float32)

    @pl.when(lat == 0)
    def _():
        f0[0] = nothing
        f1[0] = nothing
        sc[0] = nothing
        sd[0] = nothing

    @pl.when(lat == bands - 1)
    def _():
        f0[rows + 1] = nothing
        f1[rows + 1] = nothing
        sc[rows] = nothing
        sd[rows] = nothing

    def advance_row(src, dst, j, edge, beyond):
        value = src[j + 1]
        beside = jnp.concatenate([value[1:], beyond], axis=0)
        flux = ec[j] * 0.5 * (value + beside) - ed[j] * (beside - value)
        first = value[0:1]
        entering = from_west0[1, pl.ds(j, 1), :] * 0.5 * (edge + first) - from_west0[2, pl.ds(j, 1), :] * (first - edge)
        flux_west = jnp.concatenate([entering, flux[:-1]], axis=0)
        below = src[j]
        above = src[j + 2]
        flux_south = sc[j] * 0.5 * (below + value) - sd[j] * (value - below)
        flux_north = sc[j + 1] * 0.5 * (value + above) - sd[j + 1] * (above - value)
        dst[j + 1] = value - (flux - flux_west) - (flux_north - flux_south)

    def wait_z0():
        @pl.when(has_south)
        def _():
            up0.wait_recv()

        @pl.when(has_north)
        def _():
            for copy in down0:
                copy.wait_recv()

    def wait_z1(from_south):
        @pl.when(from_south)
        def _():
            up1.wait_recv()

        @pl.when(jnp.logical_not(from_south))
        def _():
            down1.wait_recv()

    @pl.when(jnp.logical_not(is_polar))
    def _():
        wait_z0()

    for copy in edges0:
        copy.wait_recv()

    def first_substep(start, stop, east_edge, west_edge):
        @pl.loop(start, stop)
        def _(t):
            j = place(t)

            @pl.when(t < rows - 1)
            def _():
                for load in load_row(place(t + 1)):
                    load.wait()

            advance_row(f0, f1, j, from_west0[0, pl.ds(j, 1), :], from_east0[pl.ds(j, 1), :])
            east_edge[pl.ds(t - start, 1), :] = f1[j + 1, width - 1 : width, :]
            west_edge[pl.ds(t - start, 1), :] = f1[j + 1, 0:1, :]

    def finish_first():
        first_substep(early, rows, to_east2, to_west2)
        for copy in edges2:
            copy.start()

        @pl.when(has_north)
        def _():
            up1.start()

        @pl.when(has_south)
        def _():
            down1.start()

    def second_early(t):
        advance_row(f1, f0, place(t), from_west1[pl.ds(t, 1), :], from_east1[pl.ds(t, 1), :])

    def second_late(t):
        late = t - early
        advance_row(f1, f0, place(t), from_west2[pl.ds(late, 1), :], from_east2[pl.ds(late, 1), :])

    first_substep(0, early, to_east1, to_west1)
    for copy in edges1:
        copy.start()

    def keep_row(j):
        return pltpu.make_async_copy(f0.at[j + 1], out.at[:, j, :], out_sem.at[j])

    def pick(table, index):
        value = table[0]
        for position in range(1, len(table)):
            value = jnp.where(index == position, table[position], value)
        return value

    def send_piece(src, index, owner):
        @pl.when(owner == me)
        def _():
            pltpu.make_async_copy(src, whole.at[me], go_send.at[index]).start()

        @pl.when(owner != me)
        def _():
            remote(src, whole.at[me], go_send.at[index], go_recv.at[me], {"lon": owner}).start()

    def filter_row(r):
        for step in range(1, parts):
            source = lax.rem(me + step, parts)
            remote(
                f0.at[1], whole.at[source], go_send.at[0], go_recv.at[source], {"lon": source}
            ).wait_recv()
        def turned(index):
            angle = 2.0 * math.pi * (index % fold) / fold
            return math.cos(angle), math.sin(angle)

        def weighted(terms):
            total = None
            for value, weight in terms:
                if abs(weight) > 1e-9:
                    term = value if abs(weight - 1.0) < 1e-9 else value * weight
                    total = term if total is None else total + term
            return total

        quarter = fold // 4
        chunks = [(start, min(48, sub - start)) for start in range(0, sub, 48)]
        for start, size in chunks:
            piece = [whole[a // 2, pl.ds((a % 2) * sub + start, size), :] for a in range(fold)]
            sums = [piece[a] + piece[a + fold // 2] for a in range(fold // 2)]
            diffs = [piece[a] - piece[a + fold // 2] for a in range(fold // 2)]
            pairs = range(1, quarter)
            even_real = [sums[a] + sums[fold // 2 - a] for a in pairs]
            even_imag = [sums[a] - sums[fold // 2 - a] for a in pairs]
            odd_real = [diffs[a] - diffs[fold // 2 - a] for a in pairs]
            odd_imag = [diffs[a] + diffs[fold // 2 - a] for a in pairs]
            space = (48 if start + 48 <= sub else tall - start) - size
            for q in range(half):
                first, cosines, sines = (
                    (sums, even_real, even_imag) if q % 2 == 0 else (diffs, odd_real, odd_imag)
                )
                real = weighted(
                    [(first[0], 1.0), (first[quarter], turned(quarter * q)[0])]
                    + [(cosines[a - 1], turned(a * q)[0]) for a in pairs]
                )
                imag = weighted(
                    [(first[quarter], -turned(quarter * q)[1])]
                    + [(sines[a - 1], -turned(a * q)[1]) for a in pairs]
                )
                here = pl.ds(start, size)
                by_cos, by_sin = tw[0, q, here, :], tw[1, q, here, :]
                if imag is None:
                    new_real, new_imag = real * by_cos, -real * by_sin
                else:
                    new_real = real * by_cos + imag * by_sin
                    new_imag = imag * by_cos - real * by_sin
                if space:
                    extra = jnp.zeros((space, 128), jnp.float32)
                    new_real = jnp.concatenate([new_real, extra], axis=0)
                    new_imag = jnp.concatenate([new_imag, extra], axis=0)
                spec[q, pl.ds(start, size + space), 0:128] = new_real
                spec[q, pl.ds(start, size + space), 128:256] = new_imag

        cut = cut_ref[pole_lat * rows + base + r].astype(jnp.float32)
        length = fold * sub

        def products(values):
            high = values.astype(jnp.bfloat16)
            low = (values - high.astype(jnp.float32)).astype(jnp.bfloat16)
            main = jnp.dot(dft[...], high, preferred_element_type=jnp.float32)
            rest = jnp.dot(dft[0 : 2 * tall, :], low, preferred_element_type=jnp.float32)
            by_cos = main[0:tall] + (main[2 * tall : 3 * tall] + rest[0:tall])
            by_sin = main[tall : 2 * tall] + (main[3 * tall : 4 * tall] + rest[tall : 2 * tall])
            return by_cos, by_sin

        @pl.loop(0, half, unroll=3)
        def _(q):
            by_cos, by_sin = products(spec[q])
            real = by_cos[:, 0:128] + by_sin[:, 128:256]
            imag = by_cos[:, 128:256] - by_sin[:, 0:128]
            wave = q + fold * lax.broadcasted_iota(jnp.int32, (tall, 128), 0)
            folded = jnp.maximum(jnp.minimum(wave, length - wave), 1).astype(jnp.float32)
            ratio = cut / folded
            damping = jnp.minimum(1.0, ratio * ratio) * (1.0 / length)
            both = jnp.concatenate([real * damping, imag * damping], axis=1)
            by_cos, by_sin = products(both)
            real = by_cos[:, 0:128] - by_sin[:, 128:256]
            imag = by_cos[:, 128:256] + by_sin[:, 0:128]
            spec[q, :, 0:128] = real * tw[0, q] - imag * tw[1, q]
            spec[q, :, 128:256] = imag * tw[0, q] + real * tw[1, q]

        for start, size in chunks:
            here = pl.ds(start, size)
            real = [spec[q, here, 0:128] * (1.0 if q in (0, half - 1) else 2.0) for q in range(half)]
            imag = [spec[q, here, 128:256] * 2.0 for q in range(half)]

            def collect(a, parity):
                waves = [q for q in range(half) if q % 2 == parity]
                in_cos = weighted([(real[q], turned(a * q)[0]) for q in waves])
                in_sin = weighted(
                    [(imag[q], turned(a * q)[1]) for q in waves if q not in (0, half - 1)]
                )
                zero = jnp.zeros((size, 128), jnp.float32)
                return zero if in_cos is None else in_cos, zero if in_sin is None else in_sin

            even, odd = [None] * (fold // 2), [None] * (fold // 2)
            for a in range(quarter + 1):
                in_cos, in_sin = collect(a, 0)
                even[a] = in_cos - in_sin
                odd_cos, odd_sin = collect(a, 1)
                odd[a] = odd_cos - odd_sin
                if 0 < a < quarter:
                    even[fold // 2 - a] = in_cos + in_sin
                    odd[fold // 2 - a] = -odd_cos - odd_sin
            for a in range(fold // 2):
                whole[a // 2, pl.ds((a % 2) * sub + start, size), :] = even[a] + odd[a]
                other = a + fold // 2
                whole[other // 2, pl.ds((other % 2) * sub + start, size), :] = even[a] - odd[a]

    def run_owner(owners, index_of, row_of, landing):
        for index, owner in enumerate(owners):
            @pl.when(owner == me)
            def _():
                pltpu.make_async_copy(f0.at[1], whole.at[me], go_send.at[index]).wait()

        owned = functools.reduce(jnp.logical_or, [owner == me for owner in owners])

        @pl.when(owned)
        def _():
            index = index_of(me)
            filter_row(row_of(index))
            for step in range(1, parts):
                target = lax.rem(me + step, parts)
                remote(
                    whole.at[target], landing(index), back_send.at[step], back_recv.at[index],
                    {"lon": target},
                ).start()
            pltpu.make_async_copy(whole.at[me], landing(index), back_recv.at[index]).start()

    def finish_owner(owners, landing):
        owned = functools.reduce(jnp.logical_or, [owner == me for owner in owners])

        @pl.when(owned)
        def _():
            for step in range(1, parts):
                target = lax.rem(me + step, parts)
                remote(
                    whole.at[target], landing(0), back_send.at[step], back_recv.at[0],
                    {"lon": target},
                ).wait_send()

    def wait_back(index, owner, landing):
        @pl.when(owner == me)
        def _():
            pltpu.make_async_copy(whole.at[me], landing(index), back_recv.at[index]).wait()

        @pl.when(owner != me)
        def _():
            remote(
                whole.at[me], landing(index), back_send.at[0], back_recv.at[index], {"lon": east}
            ).wait_recv()

    def wait_sent(index, owner, src):
        @pl.when(owner != me)
        def _():
            remote(src, whole.at[me], go_send.at[index], go_recv.at[me], {"lon": owner}).wait_send()

    def inverse(owners):
        table = [owners.index(device) if device in owners else 0 for device in range(parts)]
        return functools.partial(pick, table)

    def lend(m):
        j = base + kept + m
        return remote(f0.at[j + 1], lent.at[m], lend_send.at[m], lend_recv.at[m], {"lat": helper_lat})

    def give_back(m):
        return remote(
            lent_back.at[m], land.at[kept + m], ret_send.at[m], ret_recv.at[m],
            {"lat": pole_lat},
        )

    def kept_landing(r):
        return land.at[r]

    def store_row(r):
        return pltpu.make_async_copy(land.at[r], out.at[:, base + r, :], out_sem.at[base + r])

    def lent_landing(m):
        return lent_back.at[m]

    @pl.when(is_polar)
    def _():
        for copy in edges1:
            copy.wait_recv()

        @pl.loop(0, polar)
        def _(step):
            r = jnp.where(step < borrowed, kept + step, lax.rem(me + step - borrowed, kept))
            second_early(place(base + r))

            @pl.when(step < borrowed)
            def _():
                lend(step).start()

            @pl.when(step >= borrowed)
            def _():
                send_piece(f0.at[base + r + 1], r, pick(kept_owner, r))

        wait_z0()
        finish_first()
        second_early(polar)
        keep_row(place(polar)).start()
        wait_z1(lat > 0)
        for copy in edges2:
            copy.wait_recv()

        @pl.loop(early, rows)
        def _(t):
            second_late(t)
            keep_row(place(t)).start()

        for load in table_loads:
            load.wait()
        run_owner(kept_owner, inverse(kept_owner), lambda r: r, kept_landing)

        @pl.loop(0, kept)
        def _(r):
            wait_back(r, pick(kept_owner, r), kept_landing)
            store_row(r).start()

        @pl.loop(0, borrowed)
        def _(m):
            give_back(m).wait_recv()
            store_row(kept + m).start()

        @pl.loop(0, kept)
        def _(r):
            wait_sent(r, pick(kept_owner, r), f0.at[1])

        finish_owner(kept_owner, kept_landing)

        @pl.loop(0, borrowed)
        def _(m):
            lend(m).wait_send()

        @pl.loop(polar, rows)
        def _(t):
            keep_row(place(t)).wait()

        @pl.loop(0, polar)
        def _(r):
            store_row(r).wait()

    @pl.when(jnp.logical_not(is_polar))
    def _():
        finish_first()
        for copy in edges1 + edges2:
            copy.wait_recv()
        wait_z1(jnp.logical_not(ascending))

        @pl.loop(0, rows - 1)
        def _(step):
            t = rows - 1 - step

            @pl.when(t >= early)
            def _():
                second_late(t)

            @pl.when(t < early)
            def _():
                second_early(t)

            keep_row(place(t)).start()
            for m in range(borrowed):
                @pl.when(step == 5 + 3 * m)
                def _():
                    lend(m).wait_recv()
                    send_piece(lent.at[m], m, lent_owner[m])

        wait_z1(ascending)
        second_early(0)
        keep_row(place(0)).start()
        for load in table_loads:
            load.wait()
        run_owner(lent_owner, inverse(lent_owner), lambda m: kept + m, lent_landing)

        @pl.loop(0, borrowed)
        def _(m):
            wait_back(m, pick(lent_owner, m), lent_landing)
            give_back(m).start()

        @pl.loop(0, rows)
        def _(t):
            keep_row(t).wait()

        @pl.loop(0, borrowed)
        def _(m):
            wait_sent(m, pick(lent_owner, m), lent.at[m])
            give_back(m).wait_send()

        finish_owner(lent_owner, lent_landing)

    for copy in edges0 + edges1 + edges2:
        copy.wait_send()

    @pl.when(has_north)
    def _():
        up0.wait_send()
        up1.wait_send()

    @pl.when(has_south)
    def _():
        for copy in down0:
            copy.wait_send()
        down1.wait_send()


def share_rows(polar):
    lent = polar // 5
    return tuple(range(polar - lent)), (0, 7, 2, 4)[:lent]


def on_block(mesh, polar, tracer, east_courant, east_diffusion, south_courant, south_diffusion, cutoff):
    rows, width, levels = tracer.shape
    parts, bands = mesh.shape["lon"], mesh.shape["lat"]
    tall, half = padded(width // 2), parts + 1
    stack, twist = tables(2 * parts, width // 2)
    hbm = pl.BlockSpec(memory_space=pl.ANY)
    field = lambda count: pltpu.VMEM((count, width, levels), jnp.float32)
    edge = pltpu.VMEM((rows, levels), jnp.float32)
    edge3 = pltpu.VMEM((3, rows, levels), jnp.float32)
    kept_owner, lent_owner = share_rows(polar)
    late = pltpu.VMEM((padded(rows - polar), levels), jnp.float32)
    most = max(len(kept_owner), len(lent_owner))
    some = len(lent_owner)
    dma = lambda *shape: pltpu.SemaphoreType.DMA(shape)
    swapped = lambda values: jnp.transpose(values, (1, 0, 2))
    result = pl.pallas_call(
        functools.partial(block_kernel, rows, width, parts, bands, polar, kept_owner, lent_owner),
        out_shape=jax.ShapeDtypeStruct((width, rows, levels), jnp.float32),
        in_specs=[pl.BlockSpec(memory_space=pltpu.SMEM)] + [hbm] * 7,
        out_specs=hbm,
        scratch_shapes=[
            field(rows + 2), field(rows + 2), field(rows), field(rows), field(rows + 1), field(rows + 1),
            pltpu.VMEM(stack.shape, jnp.bfloat16),
            pltpu.VMEM(twist.shape, jnp.float32),
            field(parts),
            pltpu.VMEM((half, tall, 2 * levels), jnp.float32),
            field(some), field(some), field(polar),
            edge, edge, edge3, edge, edge, edge, late, late, late, late,
            dma(5, rows), dma(2), dma(8), dma(8), dma(6), dma(6), dma(most), dma(parts),
            dma(parts), dma(most), dma(some), dma(some), dma(some), dma(some), dma(rows),
        ],
        compiler_params=pltpu.CompilerParams(
            collective_id=0, has_side_effects=True, vmem_limit_bytes=60 * 2**20
        ),
    )(
        cutoff, swapped(tracer), swapped(east_courant), swapped(east_diffusion),
        swapped(south_courant), swapped(south_diffusion), jnp.asarray(stack), jnp.asarray(twist),
    )
    return swapped(result)


def solution(mesh):
    in_specs = (P("lat", "lon", None),) * 5 + (P(),)
    out_specs = P("lat", "lon", None)
    parts, bands = mesh.shape["lon"], mesh.shape["lat"]

    def run(tracer, *others):
        polar = tracer.shape[0] // 6
        rows = tracer.shape[0] // bands
        fits = (
            bands == 4
            and polar + SUBSTEPS < rows
            and 5 <= polar <= 10
            and tracer.shape[1] % (2 * parts) == 0
            and parts == 8
            and tracer.shape[2] == 128
        )
        body = functools.partial(on_block, mesh, polar) if fits else on_device
        return jax.shard_map(
            body, mesh=mesh, in_specs=in_specs, out_specs=out_specs, check_vma=False
        )(tracer, *others)

    return run
```

```python
import functools
import math

import jax
import jax.numpy as jnp
import ml_dtypes
import numpy as np
from jax import lax
from jax.experimental import pallas as pl
from jax.experimental.pallas import tpu as pltpu
from jax.sharding import PartitionSpec as P

SUBSTEPS = 2


def extended(block, sides, width, periodic):
    for axis, dim in sides:
        count = lax.axis_size(axis)
        forward = [(i, i + 1) for i in range(count - 1)]
        if periodic:
            forward.append((count - 1, 0))
        backward = [(target, source) for source, target in forward]
        low = lax.ppermute(
            lax.slice_in_dim(block, block.shape[dim] - width, None, axis=dim), axis, forward
        )
        high = lax.ppermute(lax.slice_in_dim(block, 0, width, axis=dim), axis, backward)
        block = jnp.concatenate([low, block, high], axis=dim)
    return block


def advance(field, east_speed, east_mix, south_speed, south_mix):
    east_flux = east_speed[:, :-1] * 0.5 * (field[:, :-1] + field[:, 1:]) - east_mix[:, :-1] * (
        field[:, 1:] - field[:, :-1]
    )
    south_flux = south_speed[1:] * 0.5 * (field[:-1] + field[1:]) - south_mix[1:] * (
        field[1:] - field[:-1]
    )
    across = east_flux[1:-1, 1:] - east_flux[1:-1, :-1]
    meridian = south_flux[1:, 1:-1] - south_flux[:-1, 1:-1]
    return field[1:-1, 1:-1] - across - meridian


def split_four(coefs, levels):
    return (
        coefs[:, :, :levels],
        coefs[:, :, levels : 2 * levels],
        coefs[:, :, 2 * levels : 3 * levels],
        coefs[:, :, 3 * levels :],
    )


def extend(values, depth):
    beside_all = extended(values, (("lon", 1),), depth, True)
    return extended(beside_all, (("lat", 0),), depth, False)


def angles(rows, cols, length):
    first = jnp.arange(rows, dtype=jnp.int32)
    second = jnp.arange(cols, dtype=jnp.int32)
    phase = first[:, None] * second[None, :] % length
    angle = phase.astype(jnp.float32) * (2.0 * math.pi / length)
    return (jnp.cos(angle), jnp.sin(angle))


def contract(form, values, table):
    return jnp.einsum(
        form, values, table, precision=lax.Precision.HIGHEST, preferred_element_type=jnp.float32
    )


def rotate(real, imag, cosine, sine, form, sign):
    new_real = contract(form, real, cosine) - sign * contract(form, imag, sine)
    new_imag = contract(form, imag, cosine) + sign * contract(form, real, sine)
    return (new_real, new_imag)


def pick_factor(length):
    factor = 1
    for candidate in range(1, int(math.isqrt(length)) + 1):
        if length % candidate == 0:
            factor = candidate
    return factor


def filter_rows_local(whole_rows, item_cut):
    share, length, levels = whole_rows.shape
    outer = pick_factor(length)
    inner = length // outer
    shaped = whole_rows.reshape(share, outer, inner, levels)
    cos_outer, sin_outer = angles(outer, outer, outer)
    cos_inner, sin_inner = angles(inner, inner, inner)
    cos_twist, sin_twist = angles(outer, inner, length)
    first_real = contract("janl,ak->jknl", shaped, cos_outer)
    first_imag = -contract("janl,ak->jknl", shaped, sin_outer)
    twist_real = cos_twist[None, :, :, None]
    twist_imag = sin_twist[None, :, :, None]
    turned_real = first_real * twist_real + first_imag * twist_imag
    turned_imag = first_imag * twist_real - first_real * twist_imag
    spec_real, spec_imag = rotate(
        turned_real, turned_imag, cos_inner, sin_inner, "jknl,nm->jkml", -1.0
    )
    low = jnp.arange(outer, dtype=jnp.int32)
    high = jnp.arange(inner, dtype=jnp.int32)
    wave = low[:, None] + outer * high[None, :]
    folded = jnp.minimum(wave, length - wave).astype(jnp.float32)
    levelled = item_cut.astype(jnp.float32)[:, None, None]
    damping = jnp.minimum(1.0, (levelled / jnp.maximum(folded, 1.0)[None, :, :]) ** 2) / length
    spec_real = spec_real * damping[:, :, :, None]
    spec_imag = spec_imag * damping[:, :, :, None]
    back_real, back_imag = rotate(spec_real, spec_imag, cos_inner, sin_inner, "jkml,nm->jknl", 1.0)
    unturned_real = back_real * twist_real - back_imag * twist_imag
    unturned_imag = back_imag * twist_real + back_real * twist_imag
    result = contract("jknl,ak->janl", unturned_real, cos_outer) - contract(
        "jknl,ak->janl", unturned_imag, sin_outer
    )
    return result.reshape(share, length, levels)


def smooth_rows(block, global_rows, cutoff):
    whole_rows = lax.all_to_all(block, "lon", split_axis=0, concat_axis=1, tiled=True)
    share = whole_rows.shape[0]
    length = whole_rows.shape[1]
    first = lax.axis_index("lon") * share
    item_row = lax.dynamic_slice_in_dim(global_rows, first, share, 0)
    matcher = item_row[:, None] == jnp.arange(cutoff.shape[0], dtype=jnp.int32)[None, :]
    item_cut = jnp.sum(jnp.where(matcher, cutoff[None, :], 0), axis=1)
    smoothed = filter_rows_local(whole_rows, item_cut)
    kept = jnp.where((item_cut < length // 2)[:, None, None], smoothed, whole_rows)
    return lax.all_to_all(kept, "lon", split_axis=1, concat_axis=0, tiled=True)


def on_device(tracer, east_courant, east_diffusion, south_courant, south_diffusion, cutoff):
    count, width, levels = tracer.shape
    lat_pos = lax.axis_index("lat")
    rows_here = lat_pos * count + jnp.arange(count, dtype=jnp.int32)
    keeper = (rows_here > 0).astype(jnp.float32)[:, None, None]
    coefs = jnp.concatenate(
        [east_courant, east_diffusion, south_courant * keeper, south_diffusion * keeper], 2
    )
    field = tracer
    coef_ext = extend(coefs, 1)
    for substep in range(SUBSTEPS):
        field = advance(extend(field, 1), *split_four(coef_ext, levels))
    field = smooth_rows(field, rows_here, cutoff)
    return field


MESH = pl.DeviceIdType.MESH


def padded(length):
    return -(-length // 16) * 16


def split_bf16(values):
    high = values.astype(ml_dtypes.bfloat16)
    low = (values - high.astype(np.float64)).astype(ml_dtypes.bfloat16)
    return high, low


def tables(parts, width):
    tall = padded(width)
    place = np.arange(width)
    angle = (place[:, None] * place[None, :] % width) * (2.0 * np.pi / width)
    stack = np.zeros((4, tall, tall), ml_dtypes.bfloat16)
    cos_high, cos_low = split_bf16(np.cos(angle))
    sin_high, sin_low = split_bf16(np.sin(angle))
    for index, table in enumerate((cos_high, sin_high, cos_low, sin_low)):
        stack[index, :width, :width] = table
    half = parts // 2 + 1
    turn = np.arange(half)[:, None] * place[None, :] * (2.0 * np.pi / (parts * width))
    twist = np.zeros((2, half, tall, 128), np.float32)
    twist[0, :, :width] = np.cos(turn)[:, :, None]
    twist[1, :, :width] = np.sin(turn)[:, :, None]
    return stack.reshape(4 * tall, tall), twist


def block_kernel(
    rows, width, parts, bands, polar, kept_owner, lent_owner,
    cut_ref, f_in, ec_in, ed_in, sc_in, sd_in, dft_in, tw_in, out,
    f0, f1, ec, ed, sc, sd, dft, tw, whole, spec, lent, lent_back, land,
    to_east1, to_west1, from_west0, from_east0, from_west1, from_east1,
    to_east2, to_west2, from_west2, from_east2,
    load_sem, table_sem, lon_send, lon_recv, z_send, z_recv, go_send, go_recv, back_send, back_recv,
    lend_send, lend_recv, ret_send, ret_recv, out_sem,
):
    me = lax.axis_index("lon")
    lat = lax.axis_index("lat")
    east = lax.rem(me + 1, parts)
    west = lax.rem(me + parts - 1, parts)
    has_south = lat > 0
    has_north = lat < bands - 1
    is_polar = jnp.logical_or(lat == 0, lat == bands - 1)
    kept, borrowed = len(kept_owner), len(lent_owner)
    ascending = lat < bands // 2
    base = jnp.where(ascending, 0, rows - polar)
    pole_lat = jnp.where(ascending, 0, bands - 1)
    helper_lat = jnp.where(ascending, 1, bands - 2)
    early = polar + 1
    fold, sub = 2 * parts, width // 2
    tall = padded(sub)
    half = fold // 2 + 1

    def place(t):
        return jnp.where(ascending, t, rows - 1 - t)

    def load_row(j):
        return [
            pltpu.make_async_copy(src.at[:, j, :], dst.at[j + shift], load_sem.at[index, j])
            for index, (src, dst, shift) in enumerate(
                ((f_in, f0, 1), (ec_in, ec, 0), (ed_in, ed, 0), (sc_in, sc, 0), (sd_in, sd, 0))
            )
        ]

    @pl.loop(0, rows)
    def _(t):
        for load in load_row(place(t)):
            load.start()

    table_loads = [
        pltpu.make_async_copy(dft_in, dft, table_sem.at[0]),
        pltpu.make_async_copy(tw_in, tw, table_sem.at[1]),
    ]
    for load in table_loads:
        load.start()

    barrier = pltpu.get_barrier_semaphore()
    for step in range(1, parts):
        pl.semaphore_signal(
            barrier, 1, device_id={"lon": lax.rem(me + step, parts)}, device_id_type=MESH
        )

    @pl.when(has_south)
    def _():
        pl.semaphore_signal(barrier, 1, device_id={"lat": lat - 1}, device_id_type=MESH)

    @pl.when(has_north)
    def _():
        pl.semaphore_signal(barrier, 1, device_id={"lat": lat + 1}, device_id_type=MESH)

    peers = parts - 1 + jnp.where(has_south, 1, 0) + jnp.where(has_north, 1, 0)
    pl.semaphore_wait(barrier, peers)

    def remote(src, dst, send, recv, where):
        return pltpu.make_async_remote_copy(
            src_ref=src, dst_ref=dst, send_sem=send, recv_sem=recv,
            device_id=where, device_id_type=MESH,
        )

    north = {"lat": lax.rem(lat + 1, bands)}
    south = {"lat": lax.rem(lat + bands - 1, bands)}
    up0 = remote(f_in.at[:, rows - 1, :], f0.at[0], z_send.at[0], z_recv.at[0], north)
    down0 = [
        remote(f_in.at[:, 0, :], f0.at[rows + 1], z_send.at[1], z_recv.at[1], south),
        remote(sc_in.at[:, 0, :], sc.at[rows], z_send.at[2], z_recv.at[2], south),
        remote(sd_in.at[:, 0, :], sd.at[rows], z_send.at[3], z_recv.at[3], south),
    ]
    up1 = remote(f1.at[rows], f1.at[0], z_send.at[4], z_recv.at[4], north)
    down1 = remote(f1.at[1], f1.at[rows + 1], z_send.at[5], z_recv.at[5], south)
    edges0 = [
        remote(f_in.at[width - 1], from_west0.at[0], lon_send.at[0], lon_recv.at[0], {"lon": east}),
        remote(ec_in.at[width - 1], from_west0.at[1], lon_send.at[1], lon_recv.at[1], {"lon": east}),
        remote(ed_in.at[width - 1], from_west0.at[2], lon_send.at[4], lon_recv.at[4], {"lon": east}),
        remote(f_in.at[0], from_east0, lon_send.at[5], lon_recv.at[5], {"lon": west}),
    ]
    edges1 = [
        remote(to_east1, from_west1, lon_send.at[2], lon_recv.at[2], {"lon": east}),
        remote(to_west1, from_east1, lon_send.at[3], lon_recv.at[3], {"lon": west}),
    ]
    edges2 = [
        remote(to_east2, from_west2, lon_send.at[6], lon_recv.at[6], {"lon": east}),
        remote(to_west2, from_east2, lon_send.at[7], lon_recv.at[7], {"lon": west}),
    ]

    for copy in edges0:
        copy.start()

    @pl.when(has_north)
    def _():
        up0.start()

    @pl.when(has_south)
    def _():
        for copy in down0:
            copy.start()

    for load in load_row(place(0)):
        load.wait()
    nothing = jnp.zeros((width, 128), jnp.float32)

    @pl.when(lat == 0)
    def _():
        f0[0] = nothing
        f1[0] = nothing
        sc[0] = nothing
        sd[0] = nothing

    @pl.when(lat == bands - 1)
    def _():
        f0[rows + 1] = nothing
        f1[rows + 1] = nothing
        sc[rows] = nothing
        sd[rows] = nothing

    def advance_row(src, dst, j, edge, beyond):
        for start in range(0, width, 48):
            size = min(48, width - start)
            here = pl.ds(start, size)
            value = src[j + 1, here, :]
            if start + size < width:
                beside = src[j + 1, pl.ds(start + 1, size), :]
            else:
                beside = jnp.concatenate([src[j + 1, pl.ds(start + 1, size - 1), :], beyond], axis=0)
            if start:
                before = pl.ds(start - 1, size)
                behind, speed_west, mix_west = src[j + 1, before, :], ec[j, before, :], ed[j, before, :]
            else:
                before = pl.ds(0, size - 1)
                behind = jnp.concatenate([edge, src[j + 1, before, :]], axis=0)
                speed_west = jnp.concatenate(
                    [from_west0[1, pl.ds(j, 1), :], ec[j, before, :]], axis=0
                )
                mix_west = jnp.concatenate([from_west0[2, pl.ds(j, 1), :], ed[j, before, :]], axis=0)
            below, above = src[j, here, :], src[j + 2, here, :]
            carried = (ec[j, here, :] * (value + beside) - speed_west * (behind + value)) + (
                sc[j + 1, here, :] * (value + above) - sc[j, here, :] * (below + value)
            )
            mixed = (ed[j, here, :] * (beside - value) - mix_west * (value - behind)) + (
                sd[j + 1, here, :] * (above - value) - sd[j, here, :] * (value - below)
            )
            dst[j + 1, here, :] = value + (mixed - 0.5 * carried)

    def wait_z0():
        @pl.when(has_south)
        def _():
            up0.wait_recv()

        @pl.when(has_north)
        def _():
            for copy in down0:
                copy.wait_recv()

    def wait_z1(from_south):
        @pl.when(from_south)
        def _():
            up1.wait_recv()

        @pl.when(jnp.logical_not(from_south))
        def _():
            down1.wait_recv()

    @pl.when(jnp.logical_not(is_polar))
    def _():
        wait_z0()

    for copy in edges0:
        copy.wait_recv()

    def first_substep(start, stop, east_edge, west_edge):
        @pl.loop(start, stop)
        def _(t):
            j = place(t)

            @pl.when(t < rows - 1)
            def _():
                for load in load_row(place(t + 1)):
                    load.wait()

            advance_row(f0, f1, j, from_west0[0, pl.ds(j, 1), :], from_east0[pl.ds(j, 1), :])
            east_edge[pl.ds(t - start, 1), :] = f1[j + 1, width - 1 : width, :]
            west_edge[pl.ds(t - start, 1), :] = f1[j + 1, 0:1, :]

    def finish_first():
        first_substep(early, rows, to_east2, to_west2)
        for copy in edges2:
            copy.start()

        @pl.when(has_north)
        def _():
            up1.start()

        @pl.when(has_south)
        def _():
            down1.start()

    def second_early(t):
        advance_row(f1, f0, place(t), from_west1[pl.ds(t, 1), :], from_east1[pl.ds(t, 1), :])

    def second_late(t):
        late = t - early
        advance_row(f1, f0, place(t), from_west2[pl.ds(late, 1), :], from_east2[pl.ds(late, 1), :])

    first_substep(0, early, to_east1, to_west1)
    for copy in edges1:
        copy.start()

    def keep_row(j):
        return pltpu.make_async_copy(f0.at[j + 1], out.at[:, j, :], out_sem.at[j])

    def pick(table, index):
        value = table[0]
        for position in range(1, len(table)):
            value = jnp.where(index == position, table[position], value)
        return value

    def send_piece(src, index, owner):
        @pl.when(owner == me)
        def _():
            pltpu.make_async_copy(src, whole.at[me], go_send.at[index]).start()

        @pl.when(owner != me)
        def _():
            remote(src, whole.at[me], go_send.at[index], go_recv.at[me], {"lon": owner}).start()

    def filter_row(r):
        for step in range(1, parts):
            source = lax.rem(me + step, parts)
            remote(
                f0.at[1], whole.at[source], go_send.at[0], go_recv.at[source], {"lon": source}
            ).wait_recv()
        def turned(index):
            angle = 2.0 * math.pi * (index % fold) / fold
            return math.cos(angle), math.sin(angle)

        def weighted(terms):
            total = None
            for value, weight in terms:
                if abs(weight) > 1e-9:
                    term = value if abs(weight - 1.0) < 1e-9 else value * weight
                    total = term if total is None else total + term
            return total

        quarter = fold // 4
        chunks = [(start, min(48, sub - start)) for start in range(0, sub, 48)]
        for start, size in chunks:
            piece = [whole[a // 2, pl.ds((a % 2) * sub + start, size), :] for a in range(fold)]
            sums = [piece[a] + piece[a + fold // 2] for a in range(fold // 2)]
            diffs = [piece[a] - piece[a + fold // 2] for a in range(fold // 2)]
            pairs = range(1, quarter)
            even_real = [sums[a] + sums[fold // 2 - a] for a in pairs]
            even_imag = [sums[a] - sums[fold // 2 - a] for a in pairs]
            odd_real = [diffs[a] - diffs[fold // 2 - a] for a in pairs]
            odd_imag = [diffs[a] + diffs[fold // 2 - a] for a in pairs]
            space = (48 if start + 48 <= sub else tall - start) - size
            for q in range(half):
                first, cosines, sines = (
                    (sums, even_real, even_imag) if q % 2 == 0 else (diffs, odd_real, odd_imag)
                )
                real = weighted(
                    [(first[0], 1.0), (first[quarter], turned(quarter * q)[0])]
                    + [(cosines[a - 1], turned(a * q)[0]) for a in pairs]
                )
                imag = weighted(
                    [(first[quarter], -turned(quarter * q)[1])]
                    + [(sines[a - 1], -turned(a * q)[1]) for a in pairs]
                )
                here = pl.ds(start, size)
                by_cos, by_sin = tw[0, q, here, :], tw[1, q, here, :]
                if imag is None:
                    new_real, new_imag = real * by_cos, -real * by_sin
                else:
                    new_real = real * by_cos + imag * by_sin
                    new_imag = imag * by_cos - real * by_sin
                if space:
                    extra = jnp.zeros((space, 128), jnp.float32)
                    new_real = jnp.concatenate([new_real, extra], axis=0)
                    new_imag = jnp.concatenate([new_imag, extra], axis=0)
                spec[q, pl.ds(start, size + space), 0:128] = new_real
                spec[q, pl.ds(start, size + space), 128:256] = new_imag

        cut = cut_ref[pole_lat * rows + base + r].astype(jnp.float32)
        length = fold * sub

        def products(values):
            high = values.astype(jnp.bfloat16)
            low = (values - high.astype(jnp.float32)).astype(jnp.bfloat16)
            main = jnp.dot(dft[...], high, preferred_element_type=jnp.float32)
            rest = jnp.dot(dft[0 : 2 * tall, :], low, preferred_element_type=jnp.float32)
            by_cos = main[0:tall] + (main[2 * tall : 3 * tall] + rest[0:tall])
            by_sin = main[tall : 2 * tall] + (main[3 * tall : 4 * tall] + rest[tall : 2 * tall])
            return by_cos, by_sin

        @pl.loop(0, half, unroll=3)
        def _(q):
            by_cos, by_sin = products(spec[q])
            real = by_cos[:, 0:128] + by_sin[:, 128:256]
            imag = by_cos[:, 128:256] - by_sin[:, 0:128]
            wave = q + fold * lax.broadcasted_iota(jnp.int32, (tall, 128), 0)
            folded = jnp.maximum(jnp.minimum(wave, length - wave), 1).astype(jnp.float32)
            ratio = cut / folded
            damping = jnp.minimum(1.0, ratio * ratio) * (1.0 / length)
            both = jnp.concatenate([real * damping, imag * damping], axis=1)
            by_cos, by_sin = products(both)
            real = by_cos[:, 0:128] - by_sin[:, 128:256]
            imag = by_cos[:, 128:256] + by_sin[:, 0:128]
            spec[q, :, 0:128] = real * tw[0, q] - imag * tw[1, q]
            spec[q, :, 128:256] = imag * tw[0, q] + real * tw[1, q]

        for start, size in chunks:
            here = pl.ds(start, size)
            real = [spec[q, here, 0:128] * (1.0 if q in (0, half - 1) else 2.0) for q in range(half)]
            imag = [spec[q, here, 128:256] * 2.0 for q in range(half)]

            def collect(a, parity):
                waves = [q for q in range(half) if q % 2 == parity]
                in_cos = weighted([(real[q], turned(a * q)[0]) for q in waves])
                in_sin = weighted(
                    [(imag[q], turned(a * q)[1]) for q in waves if q not in (0, half - 1)]
                )
                zero = jnp.zeros((size, 128), jnp.float32)
                return zero if in_cos is None else in_cos, zero if in_sin is None else in_sin

            even, odd = [None] * (fold // 2), [None] * (fold // 2)
            for a in range(quarter + 1):
                in_cos, in_sin = collect(a, 0)
                even[a] = in_cos - in_sin
                odd_cos, odd_sin = collect(a, 1)
                odd[a] = odd_cos - odd_sin
                if 0 < a < quarter:
                    even[fold // 2 - a] = in_cos + in_sin
                    odd[fold // 2 - a] = -odd_cos - odd_sin
            for a in range(fold // 2):
                whole[a // 2, pl.ds((a % 2) * sub + start, size), :] = even[a] + odd[a]
                other = a + fold // 2
                whole[other // 2, pl.ds((other % 2) * sub + start, size), :] = even[a] - odd[a]

    def run_owner(owners, index_of, row_of, landing):
        for index, owner in enumerate(owners):
            @pl.when(owner == me)
            def _():
                pltpu.make_async_copy(f0.at[1], whole.at[me], go_send.at[index]).wait()

        owned = functools.reduce(jnp.logical_or, [owner == me for owner in owners])

        @pl.when(owned)
        def _():
            index = index_of(me)
            filter_row(row_of(index))
            for step in range(1, parts):
                target = lax.rem(me + step, parts)
                remote(
                    whole.at[target], landing(index), back_send.at[step], back_recv.at[index],
                    {"lon": target},
                ).start()
            pltpu.make_async_copy(whole.at[me], landing(index), back_recv.at[index]).start()

    def finish_owner(owners, landing):
        owned = functools.reduce(jnp.logical_or, [owner == me for owner in owners])

        @pl.when(owned)
        def _():
            for step in range(1, parts):
                target = lax.rem(me + step, parts)
                remote(
                    whole.at[target], landing(0), back_send.at[step], back_recv.at[0],
                    {"lon": target},
                ).wait_send()

    def wait_back(index, owner, landing):
        @pl.when(owner == me)
        def _():
            pltpu.make_async_copy(whole.at[me], landing(index), back_recv.at[index]).wait()

        @pl.when(owner != me)
        def _():
            remote(
                whole.at[me], landing(index), back_send.at[0], back_recv.at[index], {"lon": east}
            ).wait_recv()

    def wait_sent(index, owner, src):
        @pl.when(owner != me)
        def _():
            remote(src, whole.at[me], go_send.at[index], go_recv.at[me], {"lon": owner}).wait_send()

    def inverse(owners):
        table = [owners.index(device) if device in owners else 0 for device in range(parts)]
        return functools.partial(pick, table)

    def lend(m):
        j = base + kept + m
        return remote(f0.at[j + 1], lent.at[m], lend_send.at[m], lend_recv.at[m], {"lat": helper_lat})

    def give_back(m):
        return remote(
            lent_back.at[m], land.at[kept + m], ret_send.at[m], ret_recv.at[m],
            {"lat": pole_lat},
        )

    def kept_landing(r):
        return land.at[r]

    def store_row(r):
        return pltpu.make_async_copy(land.at[r], out.at[:, base + r, :], out_sem.at[base + r])

    def lent_landing(m):
        return lent_back.at[m]

    @pl.when(is_polar)
    def _():
        for copy in edges1:
            copy.wait_recv()

        @pl.loop(0, polar)
        def _(step):
            r = jnp.where(step < borrowed, kept + step, lax.rem(me + step - borrowed, kept))
            second_early(place(base + r))

            @pl.when(step < borrowed)
            def _():
                lend(step).start()

            @pl.when(step >= borrowed)
            def _():
                send_piece(f0.at[base + r + 1], r, pick(kept_owner, r))

        wait_z0()
        finish_first()
        second_early(polar)
        keep_row(place(polar)).start()
        wait_z1(lat > 0)
        for copy in edges2:
            copy.wait_recv()

        @pl.loop(early, rows)
        def _(t):
            second_late(t)
            keep_row(place(t)).start()

        for load in table_loads:
            load.wait()
        run_owner(kept_owner, inverse(kept_owner), lambda r: r, kept_landing)

        @pl.loop(0, kept)
        def _(r):
            wait_back(r, pick(kept_owner, r), kept_landing)
            store_row(r).start()

        @pl.loop(0, borrowed)
        def _(m):
            give_back(m).wait_recv()
            store_row(kept + m).start()

        @pl.loop(0, kept)
        def _(r):
            wait_sent(r, pick(kept_owner, r), f0.at[1])

        finish_owner(kept_owner, kept_landing)

        @pl.loop(0, borrowed)
        def _(m):
            lend(m).wait_send()

        @pl.loop(polar, rows)
        def _(t):
            keep_row(place(t)).wait()

        @pl.loop(0, polar)
        def _(r):
            store_row(r).wait()

    @pl.when(jnp.logical_not(is_polar))
    def _():
        finish_first()
        for copy in edges1 + edges2:
            copy.wait_recv()
        wait_z1(jnp.logical_not(ascending))

        @pl.loop(0, rows - 1)
        def _(step):
            t = rows - 1 - step

            @pl.when(t >= early)
            def _():
                second_late(t)

            @pl.when(t < early)
            def _():
                second_early(t)

            keep_row(place(t)).start()
            for m in range(borrowed):
                @pl.when(step == 5 + 3 * m)
                def _():
                    lend(m).wait_recv()
                    send_piece(lent.at[m], m, lent_owner[m])

        for load in table_loads:
            load.wait()
        run_owner(lent_owner, inverse(lent_owner), lambda m: kept + m, lent_landing)
        wait_z1(ascending)
        second_early(0)
        keep_row(place(0)).start()

        @pl.loop(0, borrowed)
        def _(m):
            wait_back(m, pick(lent_owner, m), lent_landing)
            give_back(m).start()

        @pl.loop(0, rows)
        def _(t):
            keep_row(t).wait()

        @pl.loop(0, borrowed)
        def _(m):
            wait_sent(m, pick(lent_owner, m), lent.at[m])
            give_back(m).wait_send()

        finish_owner(lent_owner, lent_landing)

    for copy in edges0 + edges1 + edges2:
        copy.wait_send()

    @pl.when(has_north)
    def _():
        up0.wait_send()
        up1.wait_send()

    @pl.when(has_south)
    def _():
        for copy in down0:
            copy.wait_send()
        down1.wait_send()


def share_rows(polar):
    lent = polar // 5
    return tuple(range(polar - lent)), (0, 7, 2, 4)[:lent]


def on_block(mesh, polar, tracer, east_courant, east_diffusion, south_courant, south_diffusion, cutoff):
    rows, width, levels = tracer.shape
    parts, bands = mesh.shape["lon"], mesh.shape["lat"]
    tall, half = padded(width // 2), parts + 1
    stack, twist = tables(2 * parts, width // 2)
    hbm = pl.BlockSpec(memory_space=pl.ANY)
    field = lambda count: pltpu.VMEM((count, width, levels), jnp.float32)
    edge = pltpu.VMEM((rows, levels), jnp.float32)
    edge3 = pltpu.VMEM((3, rows, levels), jnp.float32)
    kept_owner, lent_owner = share_rows(polar)
    late = pltpu.VMEM((padded(rows - polar), levels), jnp.float32)
    most = max(len(kept_owner), len(lent_owner))
    some = len(lent_owner)
    dma = lambda *shape: pltpu.SemaphoreType.DMA(shape)
    swapped = lambda values: jnp.transpose(values, (1, 0, 2))
    result = pl.pallas_call(
        functools.partial(block_kernel, rows, width, parts, bands, polar, kept_owner, lent_owner),
        out_shape=jax.ShapeDtypeStruct((width, rows, levels), jnp.float32),
        in_specs=[pl.BlockSpec(memory_space=pltpu.SMEM)] + [hbm] * 7,
        out_specs=hbm,
        scratch_shapes=[
            field(rows + 2), field(rows + 2), field(rows), field(rows), field(rows + 1), field(rows + 1),
            pltpu.VMEM(stack.shape, jnp.bfloat16),
            pltpu.VMEM(twist.shape, jnp.float32),
            field(parts),
            pltpu.VMEM((half, tall, 2 * levels), jnp.float32),
            field(some), field(some), field(polar),
            edge, edge, edge3, edge, edge, edge, late, late, late, late,
            dma(5, rows), dma(2), dma(8), dma(8), dma(6), dma(6), dma(most), dma(parts),
            dma(parts), dma(most), dma(some), dma(some), dma(some), dma(some), dma(rows),
        ],
        compiler_params=pltpu.CompilerParams(
            collective_id=0, has_side_effects=True, vmem_limit_bytes=60 * 2**20
        ),
    )(
        cutoff, swapped(tracer), swapped(east_courant), swapped(east_diffusion),
        swapped(south_courant), swapped(south_diffusion), jnp.asarray(stack), jnp.asarray(twist),
    )
    return swapped(result)


def solution(mesh):
    in_specs = (P("lat", "lon", None),) * 5 + (P(),)
    out_specs = P("lat", "lon", None)
    parts, bands = mesh.shape["lon"], mesh.shape["lat"]

    def run(tracer, *others):
        polar = tracer.shape[0] // 6
        rows = tracer.shape[0] // bands
        fits = (
            bands == 4
            and polar + SUBSTEPS < rows
            and 5 <= polar <= 10
            and tracer.shape[1] % (2 * parts) == 0
            and parts == 8
            and tracer.shape[2] == 128
        )
        body = functools.partial(on_block, mesh, polar) if fits else on_device
        return jax.shard_map(
            body, mesh=mesh, in_specs=in_specs, out_specs=out_specs, check_vma=False
        )(tracer, *others)

    return run
```

```python
import functools
import math

import jax
import jax.numpy as jnp
import ml_dtypes
import numpy as np
from jax import lax
from jax.experimental import pallas as pl
from jax.experimental.pallas import tpu as pltpu
from jax.sharding import PartitionSpec as P

SUBSTEPS = 2


def extended(block, sides, width, periodic):
    for axis, dim in sides:
        count = lax.axis_size(axis)
        forward = [(i, i + 1) for i in range(count - 1)]
        if periodic:
            forward.append((count - 1, 0))
        backward = [(target, source) for source, target in forward]
        low = lax.ppermute(
            lax.slice_in_dim(block, block.shape[dim] - width, None, axis=dim), axis, forward
        )
        high = lax.ppermute(lax.slice_in_dim(block, 0, width, axis=dim), axis, backward)
        block = jnp.concatenate([low, block, high], axis=dim)
    return block


def advance(field, east_speed, east_mix, south_speed, south_mix):
    east_flux = east_speed[:, :-1] * 0.5 * (field[:, :-1] + field[:, 1:]) - east_mix[:, :-1] * (
        field[:, 1:] - field[:, :-1]
    )
    south_flux = south_speed[1:] * 0.5 * (field[:-1] + field[1:]) - south_mix[1:] * (
        field[1:] - field[:-1]
    )
    across = east_flux[1:-1, 1:] - east_flux[1:-1, :-1]
    meridian = south_flux[1:, 1:-1] - south_flux[:-1, 1:-1]
    return field[1:-1, 1:-1] - across - meridian


def split_four(coefs, levels):
    return (
        coefs[:, :, :levels],
        coefs[:, :, levels : 2 * levels],
        coefs[:, :, 2 * levels : 3 * levels],
        coefs[:, :, 3 * levels :],
    )


def extend(values, depth):
    beside_all = extended(values, (("lon", 1),), depth, True)
    return extended(beside_all, (("lat", 0),), depth, False)


def angles(rows, cols, length):
    first = jnp.arange(rows, dtype=jnp.int32)
    second = jnp.arange(cols, dtype=jnp.int32)
    phase = first[:, None] * second[None, :] % length
    angle = phase.astype(jnp.float32) * (2.0 * math.pi / length)
    return (jnp.cos(angle), jnp.sin(angle))


def contract(form, values, table):
    return jnp.einsum(
        form, values, table, precision=lax.Precision.HIGHEST, preferred_element_type=jnp.float32
    )


def rotate(real, imag, cosine, sine, form, sign):
    new_real = contract(form, real, cosine) - sign * contract(form, imag, sine)
    new_imag = contract(form, imag, cosine) + sign * contract(form, real, sine)
    return (new_real, new_imag)


def pick_factor(length):
    factor = 1
    for candidate in range(1, int(math.isqrt(length)) + 1):
        if length % candidate == 0:
            factor = candidate
    return factor


def filter_rows_local(whole_rows, item_cut):
    share, length, levels = whole_rows.shape
    outer = pick_factor(length)
    inner = length // outer
    shaped = whole_rows.reshape(share, outer, inner, levels)
    cos_outer, sin_outer = angles(outer, outer, outer)
    cos_inner, sin_inner = angles(inner, inner, inner)
    cos_twist, sin_twist = angles(outer, inner, length)
    first_real = contract("janl,ak->jknl", shaped, cos_outer)
    first_imag = -contract("janl,ak->jknl", shaped, sin_outer)
    twist_real = cos_twist[None, :, :, None]
    twist_imag = sin_twist[None, :, :, None]
    turned_real = first_real * twist_real + first_imag * twist_imag
    turned_imag = first_imag * twist_real - first_real * twist_imag
    spec_real, spec_imag = rotate(
        turned_real, turned_imag, cos_inner, sin_inner, "jknl,nm->jkml", -1.0
    )
    low = jnp.arange(outer, dtype=jnp.int32)
    high = jnp.arange(inner, dtype=jnp.int32)
    wave = low[:, None] + outer * high[None, :]
    folded = jnp.minimum(wave, length - wave).astype(jnp.float32)
    levelled = item_cut.astype(jnp.float32)[:, None, None]
    damping = jnp.minimum(1.0, (levelled / jnp.maximum(folded, 1.0)[None, :, :]) ** 2) / length
    spec_real = spec_real * damping[:, :, :, None]
    spec_imag = spec_imag * damping[:, :, :, None]
    back_real, back_imag = rotate(spec_real, spec_imag, cos_inner, sin_inner, "jkml,nm->jknl", 1.0)
    unturned_real = back_real * twist_real - back_imag * twist_imag
    unturned_imag = back_imag * twist_real + back_real * twist_imag
    result = contract("jknl,ak->janl", unturned_real, cos_outer) - contract(
        "jknl,ak->janl", unturned_imag, sin_outer
    )
    return result.reshape(share, length, levels)


def smooth_rows(block, global_rows, cutoff):
    whole_rows = lax.all_to_all(block, "lon", split_axis=0, concat_axis=1, tiled=True)
    share = whole_rows.shape[0]
    length = whole_rows.shape[1]
    first = lax.axis_index("lon") * share
    item_row = lax.dynamic_slice_in_dim(global_rows, first, share, 0)
    matcher = item_row[:, None] == jnp.arange(cutoff.shape[0], dtype=jnp.int32)[None, :]
    item_cut = jnp.sum(jnp.where(matcher, cutoff[None, :], 0), axis=1)
    smoothed = filter_rows_local(whole_rows, item_cut)
    kept = jnp.where((item_cut < length // 2)[:, None, None], smoothed, whole_rows)
    return lax.all_to_all(kept, "lon", split_axis=1, concat_axis=0, tiled=True)


def on_device(tracer, east_courant, east_diffusion, south_courant, south_diffusion, cutoff):
    count, width, levels = tracer.shape
    lat_pos = lax.axis_index("lat")
    rows_here = lat_pos * count + jnp.arange(count, dtype=jnp.int32)
    keeper = (rows_here > 0).astype(jnp.float32)[:, None, None]
    coefs = jnp.concatenate(
        [east_courant, east_diffusion, south_courant * keeper, south_diffusion * keeper], 2
    )
    field = tracer
    coef_ext = extend(coefs, 1)
    for substep in range(SUBSTEPS):
        field = advance(extend(field, 1), *split_four(coef_ext, levels))
    field = smooth_rows(field, rows_here, cutoff)
    return field


MESH = pl.DeviceIdType.MESH


def padded(length):
    return -(-length // 16) * 16


def split_bf16(values):
    high = values.astype(ml_dtypes.bfloat16)
    low = (values - high.astype(np.float64)).astype(ml_dtypes.bfloat16)
    return high, low


def tables(parts, width):
    tall = padded(width)
    place = np.arange(width)
    angle = (place[:, None] * place[None, :] % width) * (2.0 * np.pi / width)
    stack = np.zeros((4, tall, tall), ml_dtypes.bfloat16)
    cos_high, cos_low = split_bf16(np.cos(angle))
    sin_high, sin_low = split_bf16(np.sin(angle))
    for index, table in enumerate((cos_high, sin_high, cos_low, sin_low)):
        stack[index, :width, :width] = table
    half = parts // 2 + 1
    turn = np.arange(half)[:, None] * place[None, :] * (2.0 * np.pi / (parts * width))
    twist = np.zeros((2, half, tall, 128), np.float32)
    twist[0, :, :width] = np.cos(turn)[:, :, None]
    twist[1, :, :width] = np.sin(turn)[:, :, None]
    return stack.reshape(4 * tall, tall), twist


def block_kernel(
    rows, width, parts, bands, polar, kept_owner, lent_owner,
    cut_ref, f_in, ec_in, ed_in, sc_in, sd_in, dft_in, tw_in, out,
    f0, f1, ec, ed, sc, sd, dft, tw, whole, spec, lent, lent_back, land,
    from_west0, from_east0, to_east1, to_west1, from_west1, from_east1,
    load_sem, table_sem, lon_send, lon_recv, z_send, z_recv, go_send, go_recv, back_send, back_recv,
    lend_send, lend_recv, ret_send, ret_recv, out_sem, edge_send, edge_recv,
):
    me = lax.axis_index("lon")
    lat = lax.axis_index("lat")
    east = lax.rem(me + 1, parts)
    west = lax.rem(me + parts - 1, parts)
    has_south = lat > 0
    has_north = lat < bands - 1
    is_polar = jnp.logical_or(lat == 0, lat == bands - 1)
    kept, borrowed = len(kept_owner), len(lent_owner)
    ascending = lat < bands // 2
    base = jnp.where(ascending, 0, rows - polar)
    pole_lat = jnp.where(ascending, 0, bands - 1)
    helper_lat = jnp.where(ascending, 1, bands - 2)
    groups = rows // 4
    fold, sub = 2 * parts, width // 2
    tall = padded(sub)
    half = fold // 2 + 1

    def place(t):
        return jnp.where(ascending, t, rows - 1 - t)

    def load_row(j):
        return [
            pltpu.make_async_copy(src.at[:, j, :], dst.at[j + shift], load_sem.at[index, j])
            for index, (src, dst, shift) in enumerate(
                ((f_in, f0, 1), (ec_in, ec, 0), (ed_in, ed, 0), (sc_in, sc, 0), (sd_in, sd, 0))
            )
        ]

    @pl.loop(0, rows)
    def _(t):
        for load in load_row(place(t)):
            load.start()

    table_loads = [
        pltpu.make_async_copy(dft_in, dft, table_sem.at[0]),
        pltpu.make_async_copy(tw_in, tw, table_sem.at[1]),
    ]
    for load in table_loads:
        load.start()

    barrier = pltpu.get_barrier_semaphore()
    for step in range(1, parts):
        pl.semaphore_signal(
            barrier, 1, device_id={"lon": lax.rem(me + step, parts)}, device_id_type=MESH
        )

    @pl.when(has_south)
    def _():
        pl.semaphore_signal(barrier, 1, device_id={"lat": lat - 1}, device_id_type=MESH)

    @pl.when(has_north)
    def _():
        pl.semaphore_signal(barrier, 1, device_id={"lat": lat + 1}, device_id_type=MESH)

    peers = parts - 1 + jnp.where(has_south, 1, 0) + jnp.where(has_north, 1, 0)
    pl.semaphore_wait(barrier, peers)

    def remote(src, dst, send, recv, where):
        return pltpu.make_async_remote_copy(
            src_ref=src, dst_ref=dst, send_sem=send, recv_sem=recv,
            device_id=where, device_id_type=MESH,
        )

    north = {"lat": lax.rem(lat + 1, bands)}
    south = {"lat": lax.rem(lat + bands - 1, bands)}
    up0 = remote(f_in.at[:, rows - 1, :], f0.at[0], z_send.at[0], z_recv.at[0], north)
    down0 = [
        remote(f_in.at[:, 0, :], f0.at[rows + 1], z_send.at[1], z_recv.at[1], south),
        remote(sc_in.at[:, 0, :], sc.at[rows], z_send.at[2], z_recv.at[2], south),
        remote(sd_in.at[:, 0, :], sd.at[rows], z_send.at[3], z_recv.at[3], south),
    ]
    up1 = remote(f1.at[rows], f1.at[0], z_send.at[4], z_recv.at[4], north)
    down1 = remote(f1.at[1], f1.at[rows + 1], z_send.at[5], z_recv.at[5], south)
    edges0 = [
        remote(f_in.at[width - 1], from_west0.at[0], lon_send.at[0], lon_recv.at[0], {"lon": east}),
        remote(ec_in.at[width - 1], from_west0.at[1], lon_send.at[1], lon_recv.at[1], {"lon": east}),
        remote(ed_in.at[width - 1], from_west0.at[2], lon_send.at[4], lon_recv.at[4], {"lon": east}),
        remote(f_in.at[0], from_east0, lon_send.at[5], lon_recv.at[5], {"lon": west}),
    ]
    edges1 = [
        (
            remote(to_east1.at[g], from_west1.at[g], edge_send.at[0, g], edge_recv.at[0, g], {"lon": east}),
            remote(to_west1.at[g], from_east1.at[g], edge_send.at[1, g], edge_recv.at[1, g], {"lon": west}),
        )
        for g in range(groups)
    ]

    for copy in edges0:
        copy.start()

    @pl.when(has_north)
    def _():
        up0.start()

    @pl.when(has_south)
    def _():
        for copy in down0:
            copy.start()

    for load in load_row(place(0)):
        load.wait()
    nothing = jnp.zeros((width, 128), jnp.float32)

    @pl.when(lat == 0)
    def _():
        f0[0] = nothing
        f1[0] = nothing
        sc[0] = nothing
        sd[0] = nothing

    @pl.when(lat == bands - 1)
    def _():
        f0[rows + 1] = nothing
        f1[rows + 1] = nothing
        sc[rows] = nothing
        sd[rows] = nothing

    def advance_row(src, dst, j, edge, beyond):
        for start in range(0, width, 48):
            size = min(48, width - start)
            here = pl.ds(start, size)
            value = src[j + 1, here, :]
            if start + size < width:
                beside = src[j + 1, pl.ds(start + 1, size), :]
            else:
                beside = jnp.concatenate([src[j + 1, pl.ds(start + 1, size - 1), :], beyond], axis=0)
            if start:
                before = pl.ds(start - 1, size)
                behind, speed_west, mix_west = src[j + 1, before, :], ec[j, before, :], ed[j, before, :]
            else:
                before = pl.ds(0, size - 1)
                behind = jnp.concatenate([edge, src[j + 1, before, :]], axis=0)
                speed_west = jnp.concatenate(
                    [from_west0[1, pl.ds(j, 1), :], ec[j, before, :]], axis=0
                )
                mix_west = jnp.concatenate([from_west0[2, pl.ds(j, 1), :], ed[j, before, :]], axis=0)
            below, above = src[j, here, :], src[j + 2, here, :]
            carried = (ec[j, here, :] * (value + beside) - speed_west * (behind + value)) + (
                sc[j + 1, here, :] * (value + above) - sc[j, here, :] * (below + value)
            )
            mixed = (ed[j, here, :] * (beside - value) - mix_west * (value - behind)) + (
                sd[j + 1, here, :] * (above - value) - sd[j, here, :] * (value - below)
            )
            dst[j + 1, here, :] = value + (mixed - 0.5 * carried)

    def wait_z0():
        @pl.when(has_south)
        def _():
            up0.wait_recv()

        @pl.when(has_north)
        def _():
            for copy in down0:
                copy.wait_recv()

    def wait_z1(from_south):
        @pl.when(from_south)
        def _():
            up1.wait_recv()

        @pl.when(jnp.logical_not(from_south))
        def _():
            down1.wait_recv()

    @pl.when(jnp.logical_not(is_polar))
    def _():
        wait_z0()

    for copy in edges0:
        copy.wait_recv()

    def first_group(group):
        @pl.loop(4 * group, 4 * group + 4)
        def _(t):
            j = place(t)

            @pl.when(t < rows - 1)
            def _():
                for load in load_row(place(t + 1)):
                    load.wait()

            advance_row(f0, f1, j, from_west0[0, pl.ds(j, 1), :], from_east0[pl.ds(j, 1), :])
            to_east1[group, pl.ds(t - 4 * group, 1), :] = f1[j + 1, width - 1 : width, :]
            to_west1[group, pl.ds(t - 4 * group, 1), :] = f1[j + 1, 0:1, :]

        for copy in edges1[group]:
            copy.start()

    def wait_group(group):
        for copy in edges1[group]:
            copy.wait_recv()

    def send_z1():
        @pl.when(has_north)
        def _():
            up1.start()

        @pl.when(has_south)
        def _():
            down1.start()

    def second(t):
        group, spot = t // 4, pl.ds(t % 4, 1)
        advance_row(f1, f0, place(t), from_west1[group, spot, :], from_east1[group, spot, :])

    def keep_row(j):
        return pltpu.make_async_copy(f0.at[j + 1], out.at[:, j, :], out_sem.at[j])

    def pick(table, index):
        value = table[0]
        for position in range(1, len(table)):
            value = jnp.where(index == position, table[position], value)
        return value

    def send_piece(src, index, owner):
        @pl.when(owner == me)
        def _():
            pltpu.make_async_copy(src, whole.at[me], go_send.at[index]).start()

        @pl.when(owner != me)
        def _():
            remote(src, whole.at[me], go_send.at[index], go_recv.at[me], {"lon": owner}).start()

    def filter_row(r):
        for step in range(1, parts):
            source = lax.rem(me + step, parts)
            remote(
                f0.at[1], whole.at[source], go_send.at[0], go_recv.at[source], {"lon": source}
            ).wait_recv()
        def turned(index):
            angle = 2.0 * math.pi * (index % fold) / fold
            return math.cos(angle), math.sin(angle)

        def weighted(terms):
            total = None
            for value, weight in terms:
                if abs(weight) > 1e-9:
                    term = value if abs(weight - 1.0) < 1e-9 else value * weight
                    total = term if total is None else total + term
            return total

        quarter = fold // 4
        chunks = [(start, min(48, sub - start)) for start in range(0, sub, 48)]
        for start, size in chunks:
            piece = [whole[a // 2, pl.ds((a % 2) * sub + start, size), :] for a in range(fold)]
            sums = [piece[a] + piece[a + fold // 2] for a in range(fold // 2)]
            diffs = [piece[a] - piece[a + fold // 2] for a in range(fold // 2)]
            pairs = range(1, quarter)
            even_real = [sums[a] + sums[fold // 2 - a] for a in pairs]
            even_imag = [sums[a] - sums[fold // 2 - a] for a in pairs]
            odd_real = [diffs[a] - diffs[fold // 2 - a] for a in pairs]
            odd_imag = [diffs[a] + diffs[fold // 2 - a] for a in pairs]
            space = (48 if start + 48 <= sub else tall - start) - size
            for q in range(half):
                first, cosines, sines = (
                    (sums, even_real, even_imag) if q % 2 == 0 else (diffs, odd_real, odd_imag)
                )
                real = weighted(
                    [(first[0], 1.0), (first[quarter], turned(quarter * q)[0])]
                    + [(cosines[a - 1], turned(a * q)[0]) for a in pairs]
                )
                imag = weighted(
                    [(first[quarter], -turned(quarter * q)[1])]
                    + [(sines[a - 1], -turned(a * q)[1]) for a in pairs]
                )
                here = pl.ds(start, size)
                by_cos, by_sin = tw[0, q, here, :], tw[1, q, here, :]
                if imag is None:
                    new_real, new_imag = real * by_cos, -real * by_sin
                else:
                    new_real = real * by_cos + imag * by_sin
                    new_imag = imag * by_cos - real * by_sin
                if space:
                    extra = jnp.zeros((space, 128), jnp.float32)
                    new_real = jnp.concatenate([new_real, extra], axis=0)
                    new_imag = jnp.concatenate([new_imag, extra], axis=0)
                spec[q, pl.ds(start, size + space), 0:128] = new_real
                spec[q, pl.ds(start, size + space), 128:256] = new_imag

        cut = cut_ref[pole_lat * rows + place(r)].astype(jnp.float32)
        length = fold * sub

        def products(values):
            high = values.astype(jnp.bfloat16)
            low = (values - high.astype(jnp.float32)).astype(jnp.bfloat16)
            main = jnp.dot(dft[...], high, preferred_element_type=jnp.float32)
            rest = jnp.dot(dft[0 : 2 * tall, :], low, preferred_element_type=jnp.float32)
            by_cos = main[0:tall] + (main[2 * tall : 3 * tall] + rest[0:tall])
            by_sin = main[tall : 2 * tall] + (main[3 * tall : 4 * tall] + rest[tall : 2 * tall])
            return by_cos, by_sin

        @pl.loop(0, half, unroll=3)
        def _(q):
            by_cos, by_sin = products(spec[q])
            real = by_cos[:, 0:128] + by_sin[:, 128:256]
            imag = by_cos[:, 128:256] - by_sin[:, 0:128]
            wave = q + fold * lax.broadcasted_iota(jnp.int32, (tall, 128), 0)
            folded = jnp.maximum(jnp.minimum(wave, length - wave), 1).astype(jnp.float32)
            ratio = cut / folded
            damping = jnp.minimum(1.0, ratio * ratio) * (1.0 / length)
            both = jnp.concatenate([real * damping, imag * damping], axis=1)
            by_cos, by_sin = products(both)
            real = by_cos[:, 0:128] - by_sin[:, 128:256]
            imag = by_cos[:, 128:256] + by_sin[:, 0:128]
            spec[q, :, 0:128] = real * tw[0, q] - imag * tw[1, q]
            spec[q, :, 128:256] = imag * tw[0, q] + real * tw[1, q]

        for start, size in chunks:
            here = pl.ds(start, size)
            real = [spec[q, here, 0:128] * (1.0 if q in (0, half - 1) else 2.0) for q in range(half)]
            imag = [spec[q, here, 128:256] * 2.0 for q in range(half)]

            def collect(a, parity):
                waves = [q for q in range(half) if q % 2 == parity]
                in_cos = weighted([(real[q], turned(a * q)[0]) for q in waves])
                in_sin = weighted(
                    [(imag[q], turned(a * q)[1]) for q in waves if q not in (0, half - 1)]
                )
                zero = jnp.zeros((size, 128), jnp.float32)
                return zero if in_cos is None else in_cos, zero if in_sin is None else in_sin

            even, odd = [None] * (fold // 2), [None] * (fold // 2)
            for a in range(quarter + 1):
                in_cos, in_sin = collect(a, 0)
                even[a] = in_cos - in_sin
                odd_cos, odd_sin = collect(a, 1)
                odd[a] = odd_cos - odd_sin
                if 0 < a < quarter:
                    even[fold // 2 - a] = in_cos + in_sin
                    odd[fold // 2 - a] = -odd_cos - odd_sin
            for a in range(fold // 2):
                whole[a // 2, pl.ds((a % 2) * sub + start, size), :] = even[a] + odd[a]
                other = a + fold // 2
                whole[other // 2, pl.ds((other % 2) * sub + start, size), :] = even[a] - odd[a]

    def run_owner(owners, index_of, row_of, landing):
        for index, owner in enumerate(owners):
            @pl.when(owner == me)
            def _():
                pltpu.make_async_copy(f0.at[1], whole.at[me], go_send.at[index]).wait()

        owned = functools.reduce(jnp.logical_or, [owner == me for owner in owners])

        @pl.when(owned)
        def _():
            index = index_of(me)
            filter_row(row_of(index))
            for step in range(1, parts):
                target = lax.rem(me + step, parts)
                remote(
                    whole.at[target], landing(index), back_send.at[step], back_recv.at[index],
                    {"lon": target},
                ).start()
            pltpu.make_async_copy(whole.at[me], landing(index), back_recv.at[index]).start()

    def finish_owner(owners, landing):
        owned = functools.reduce(jnp.logical_or, [owner == me for owner in owners])

        @pl.when(owned)
        def _():
            for step in range(1, parts):
                target = lax.rem(me + step, parts)
                remote(
                    whole.at[target], landing(0), back_send.at[step], back_recv.at[0],
                    {"lon": target},
                ).wait_send()

    def wait_back(index, owner, landing):
        @pl.when(owner == me)
        def _():
            pltpu.make_async_copy(whole.at[me], landing(index), back_recv.at[index]).wait()

        @pl.when(owner != me)
        def _():
            remote(
                whole.at[me], landing(index), back_send.at[0], back_recv.at[index], {"lon": east}
            ).wait_recv()

    def wait_sent(index, owner, src):
        @pl.when(owner != me)
        def _():
            remote(src, whole.at[me], go_send.at[index], go_recv.at[me], {"lon": owner}).wait_send()

    def inverse(owners):
        table = [owners.index(device) if device in owners else 0 for device in range(parts)]
        return functools.partial(pick, table)

    def lend(m):
        j = place(m)
        return remote(f0.at[j + 1], lent.at[m], lend_send.at[m], lend_recv.at[m], {"lat": helper_lat})

    def give_back(m):
        return remote(
            lent_back.at[m], land.at[kept + m], ret_send.at[m], ret_recv.at[m],
            {"lat": pole_lat},
        )

    def kept_landing(r):
        return land.at[r]

    def store_row(index):
        j = place(jnp.where(index < kept, borrowed + index, index - kept))
        return pltpu.make_async_copy(land.at[index], out.at[:, j, :], out_sem.at[j])

    def lent_landing(m):
        return lent_back.at[m]

    @pl.when(is_polar)
    def _():
        def leave(start, stop):
            count = stop - start

            @pl.loop(0, count)
            def _(step):
                t = start + lax.rem(me // 2 + step, count) if start >= borrowed else start + step
                second(t)

                @pl.when(t < borrowed)
                def _():
                    lend(jnp.minimum(t, borrowed - 1)).start()

                @pl.when(t >= borrowed)
                def _():
                    index = jnp.maximum(t - borrowed, 0)
                    send_piece(f0.at[place(t) + 1], index, pick(kept_owner, index))

        last = (polar + 3) // 4
        for group in range(last):
            first_group(group)
            if group:
                wait_group(group - 1)
                leave(4 * group - 4, 4 * group)
        wait_group(last - 1)
        leave(4 * last - 4, polar)
        wait_z0()
        for group in range(last, groups):
            first_group(group)
        send_z1()
        for group in range(last, groups):
            wait_group(group)

        @pl.loop(polar, rows - 1)
        def _(t):
            second(t)
            keep_row(place(t)).start()

        wait_z1(lat > 0)
        second(rows - 1)
        keep_row(place(rows - 1)).start()
        for load in table_loads:
            load.wait()
        run_owner(kept_owner, inverse(kept_owner), lambda r: borrowed + r, kept_landing)

        @pl.loop(0, kept)
        def _(r):
            wait_back(r, pick(kept_owner, r), kept_landing)
            store_row(r).start()

        @pl.loop(0, borrowed)
        def _(m):
            give_back(m).wait_recv()
            store_row(kept + m).start()

        @pl.loop(0, kept)
        def _(r):
            wait_sent(r, pick(kept_owner, r), f0.at[1])

        finish_owner(kept_owner, kept_landing)

        @pl.loop(0, borrowed)
        def _(m):
            lend(m).wait_send()

        @pl.loop(polar, rows)
        def _(t):
            keep_row(place(t)).wait()

        @pl.loop(0, polar)
        def _(index):
            store_row(index).wait()

    @pl.when(jnp.logical_not(is_polar))
    def _():
        for group in range(groups):
            first_group(group)
        send_z1()
        for group in range(groups):
            wait_group(group)
        wait_z1(jnp.logical_not(ascending))

        @pl.loop(0, rows - 1)
        def _(step):
            t = rows - 1 - step

            second(t)
            keep_row(place(t)).start()
            for m in range(borrowed):
                @pl.when(step == 5 + 3 * m)
                def _():
                    lend(m).wait_recv()
                    send_piece(lent.at[m], m, lent_owner[m])

        for load in table_loads:
            load.wait()
        run_owner(lent_owner, inverse(lent_owner), lambda m: m, lent_landing)
        wait_z1(ascending)
        second(0)
        keep_row(place(0)).start()

        @pl.loop(0, borrowed)
        def _(m):
            wait_back(m, pick(lent_owner, m), lent_landing)
            give_back(m).start()

        @pl.loop(0, rows)
        def _(t):
            keep_row(t).wait()

        @pl.loop(0, borrowed)
        def _(m):
            wait_sent(m, pick(lent_owner, m), lent.at[m])
            give_back(m).wait_send()

        finish_owner(lent_owner, lent_landing)

    for copy in edges0 + [copy for pair in edges1 for copy in pair]:
        copy.wait_send()

    @pl.when(has_north)
    def _():
        up0.wait_send()
        up1.wait_send()

    @pl.when(has_south)
    def _():
        for copy in down0:
            copy.wait_send()
        down1.wait_send()


def share_rows(polar):
    lent = polar // 5
    return (0, 2, 4, 6, 1, 3, 5, 7)[: polar - lent], (0, 7, 2, 4)[:lent]


def on_block(mesh, polar, tracer, east_courant, east_diffusion, south_courant, south_diffusion, cutoff):
    rows, width, levels = tracer.shape
    parts, bands = mesh.shape["lon"], mesh.shape["lat"]
    tall, half = padded(width // 2), parts + 1
    stack, twist = tables(2 * parts, width // 2)
    hbm = pl.BlockSpec(memory_space=pl.ANY)
    field = lambda count: pltpu.VMEM((count, width, levels), jnp.float32)
    edge = pltpu.VMEM((rows, levels), jnp.float32)
    edge3 = pltpu.VMEM((3, rows, levels), jnp.float32)
    kept_owner, lent_owner = share_rows(polar)
    batch = pltpu.VMEM((rows // 4, 8, levels), jnp.float32)
    most = max(len(kept_owner), len(lent_owner))
    some = len(lent_owner)
    dma = lambda *shape: pltpu.SemaphoreType.DMA(shape)
    swapped = lambda values: jnp.transpose(values, (1, 0, 2))
    result = pl.pallas_call(
        functools.partial(block_kernel, rows, width, parts, bands, polar, kept_owner, lent_owner),
        out_shape=jax.ShapeDtypeStruct((width, rows, levels), jnp.float32),
        in_specs=[pl.BlockSpec(memory_space=pltpu.SMEM)] + [hbm] * 7,
        out_specs=hbm,
        scratch_shapes=[
            field(rows + 2), field(rows + 2), field(rows), field(rows), field(rows + 1), field(rows + 1),
            pltpu.VMEM(stack.shape, jnp.bfloat16),
            pltpu.VMEM(twist.shape, jnp.float32),
            field(parts),
            pltpu.VMEM((half, tall, 2 * levels), jnp.float32),
            field(some), field(some), field(polar),
            edge3, edge, batch, batch, batch, batch,
            dma(5, rows), dma(2), dma(8), dma(8), dma(6), dma(6), dma(most), dma(parts),
            dma(parts), dma(most), dma(some), dma(some), dma(some), dma(some), dma(rows), dma(2, rows // 4), dma(2, rows // 4),
        ],
        compiler_params=pltpu.CompilerParams(
            collective_id=0, has_side_effects=True, vmem_limit_bytes=60 * 2**20
        ),
    )(
        cutoff, swapped(tracer), swapped(east_courant), swapped(east_diffusion),
        swapped(south_courant), swapped(south_diffusion), jnp.asarray(stack), jnp.asarray(twist),
    )
    return swapped(result)


def solution(mesh):
    in_specs = (P("lat", "lon", None),) * 5 + (P(),)
    out_specs = P("lat", "lon", None)
    parts, bands = mesh.shape["lon"], mesh.shape["lat"]

    def run(tracer, *others):
        polar = tracer.shape[0] // 6
        rows = tracer.shape[0] // bands
        fits = (
            bands == 4
            and polar + SUBSTEPS < rows
            and 5 <= polar <= 10
            and tracer.shape[1] % (2 * parts) == 0
            and parts == 8
            and rows % 4 == 0
            and -(-polar // 4) * 4 < rows
            and tracer.shape[2] == 128
        )
        body = functools.partial(on_block, mesh, polar) if fits else on_device
        return jax.shard_map(
            body, mesh=mesh, in_specs=in_specs, out_specs=out_specs, check_vma=False
        )(tracer, *others)

    return run
```
